512 devices in a mesh: aux: 128 (over z, y, core), orb: 4 (over x).
Axes of the slice: x: 4, y: 8, z: 8, core: 2. Of those that a mesh axis runs over, the one named last changes fastest.
Arguments:
- half_integrals: bfloat16 [128, 32768, 128], P('orb', 'aux'), may hold values from -1.11488167 to 1.11488167
- domain_map: bfloat16 [128, 128, 128], P('orb'), may hold values from -0.5 to 0.5
- domain_index: int32 [128, 128], replicated, may hold values from -1 to 24999, as said below
- owner_orbitals: int32 [128, 4], replicated, may hold values from 0 to 127, as said below
- pair_slots: int32 [2048, 2], P('aux'), may hold values from 0 to 3, as said below
- pair_weight: int32 [2048], P('aux'), may hold values from 0 to 2, as said below
- virtual_energy: float32 [25000], replicated, may hold values from 0.2 to 3
- occupied_energy: float32 [128], replicated, may hold values from -2 to -0.5
Outputs:
- amplitude: bfloat16 [2048, 128, 128], P(('aux', 'orb'))
- pair_energy: float32 [2048], P(('aux', 'orb'))
- domain_grad: float32 [128, 128], P('orb')
The draws below stay inside these ranges and needn't reach their ends.
Inputs may be any that keep to these rules, and one draw needn't show every extreme that they name: `domain_index`: each orbital's live slots come first and the rest are -1; some orbital's domain has all 128 slots live. `owner_orbitals`: entry g (g = 0 to 3) of an owner's list is an orbital of group g, that is g * 32 to (g + 1) * 32 - 1; the entries of one owner are distinct. `pair_slots`: the two positions of a row may be equal; no ordered pair of positions stands twice among one owner's rows. `pair_weight`: in each owner's 16 rows the live pairs (weight 1 or 2) come first and the rest have weight 0; every owner has a live pair and some owner has all 16 live.
All inputs are finite; a program needn't handle non-finite values.
Results may differ from the reference program's by a relative error of at most 0.0034.
Values may be sent and summed in bfloat16 or wider, within the bound.
No kernel may reach another device: no remote copies, remote signals or barrier semaphores. Data moves between devices by JAX's collectives and lax.ppermute only.
A program may use at most 64 MiB of HBM per device.

```python
import math
import jax
import jax.numpy as jnp
from jax import lax

DOM = 128
AUX_DEV = 256
NVIRT = 25000
OCC_DEV = 32
OWN_GRP = 1
PAIR_CAP = 16
NAUX = 32768
NOCC = 128
OWNERS = 128
M = 4
NPAIRS = 2048


def draw_half_integrals(key, part):
    key = jax.random.fold_in(key, 11)
    key_own = jax.random.fold_in(key, 0)
    key_common = jax.random.fold_in(key, 1)
    key_block = jax.random.fold_in(key, 3)
    key_top = jax.random.fold_in(key, 4)
    shape = (NOCC, NAUX, DOM)
    factor = float(NAUX) ** (-0.25)
    block_count = NAUX // AUX_DEV
    block_scale = jnp.exp(jax.random.uniform(key_block, (block_count,), jnp.float32, 0.0, 2.9957323))
    top_block = jax.random.randint(key_top, (), 0, block_count)
    block_scale = jnp.where(jnp.arange(block_count) == top_block, jnp.float32(20.0), block_scale)
    block_scale = block_scale / 8.1618
    row_scale = jnp.repeat(block_scale, AUX_DEV)[None, :, None]
    own = jax.random.normal(key_own, shape, jnp.float32)
    common = jax.random.normal(key_common, (1, NAUX, DOM), jnp.float32)
    values = 0.8 * common + 0.6 * own
    values = jnp.clip(values * row_scale, -15.0, 15.0)
    return (values * factor).astype(jnp.bfloat16)


def draw_domain_index(key, part):
    key = jax.random.fold_in(key, 12)
    key_len, key_full, key_idx = jax.random.split(key, 3)
    lengths = jax.random.randint(key_len, (NOCC,), DOM // 3, DOM + 1)
    full_orb = jax.random.randint(key_full, (), 0, NOCC)
    lengths = jnp.where(jnp.arange(NOCC) == full_orb, DOM, lengths)
    picked = jax.random.randint(key_idx, (NOCC, DOM), 0, NVIRT)
    return jnp.where(jnp.arange(DOM)[None, :] < lengths[:, None], picked, -1).astype(jnp.int32)


def draw_owner_orbitals(key, part):
    key = jax.random.fold_in(key, 13)
    groups_count = M // OWN_GRP
    scores = jax.random.randint(key, (OWNERS, groups_count, OCC_DEV), 0, 2 ** 20) * OCC_DEV + jnp.arange(OCC_DEV)
    chosen = jnp.argsort(scores, axis=-1, stable=True)[:, :, :OWN_GRP]
    chosen = chosen + (jnp.arange(groups_count) * OCC_DEV)[None, :, None]
    return chosen.reshape(OWNERS, M).astype(jnp.int32)


def draw_pair_slots(key, part):
    key = jax.random.fold_in(key, 14)
    combos = M * M
    codes = jnp.arange(combos)
    scores = jax.random.randint(key, (OWNERS, combos), 0, 2 ** 20) * combos + codes
    chosen = jnp.argsort(scores, axis=-1, stable=True)[:, :PAIR_CAP]
    slot_pair = jnp.stack([chosen // M, chosen % M], axis=-1)
    return slot_pair.reshape(OWNERS * PAIR_CAP, 2).astype(jnp.int32)


def draw_pair_weight(key, part):
    key = jax.random.fold_in(key, 15)
    key_count, key_full, key_weight = jax.random.split(key, 3)
    counts = jax.random.randint(key_count, (OWNERS,), 1, PAIR_CAP + 1)
    full_owner = jax.random.randint(key_full, (), 0, OWNERS)
    counts = jnp.where(jnp.arange(OWNERS) == full_owner, PAIR_CAP, counts)
    weights = jax.random.randint(key_weight, (OWNERS, PAIR_CAP), 1, 3)
    weights = jnp.where(jnp.arange(PAIR_CAP)[None, :] < counts[:, None], weights, 0)
    return weights.reshape(OWNERS * PAIR_CAP).astype(jnp.int32)


def block_levels(rng, dims, cuts, smallest, high):
    factor_of, own = 1.0, jax.random.fold_in(rng, 6)
    for dim, parts in cuts:
        steps = jnp.exp(jax.random.uniform(jax.random.fold_in(own, dim), (parts,), jnp.float32, smallest / len(cuts), high / len(cuts)))
        factor_of = factor_of * jnp.repeat(steps, dims[dim] // parts).reshape([-1 if axis == dim else 1 for axis in range(len(dims))])
    return factor_of


def gaussian(own_key, shape, deviation, reach, shards=(), kind=jnp.bfloat16):
    entries = deviation * jax.random.normal(own_key, shape, jnp.float32)
    if shards:
        entries = entries * block_levels(own_key, shape, shards, -0.22, 0.18)
    return jnp.clip(entries, -reach, reach).astype(kind)


def setup_inputs(seed: int = 0) -> dict:
    key_of = jax.random.split(jax.random.key(seed), 9)
    half_integrals = draw_half_integrals(jax.random.fold_in(key_of[8], 71), 0)
    domain_map = gaussian(key_of[1], (NOCC, DOM, DOM), DOM ** -0.5, 0.5, ((0, 4),))
    domain_index = draw_domain_index(jax.random.fold_in(key_of[8], 71), 0)
    owner_orbitals = draw_owner_orbitals(jax.random.fold_in(key_of[8], 71), 0)
    pair_slots = draw_pair_slots(jax.random.fold_in(key_of[8], 71), 0)
    pair_weight = draw_pair_weight(jax.random.fold_in(key_of[8], 71), 0)
    virtual_energy = jnp.clip(jnp.exp(jax.random.uniform(key_of[6], (NVIRT,), jnp.float32, math.log(0.2), math.log(3.0))), 0.2, 3.0)
    occupied_energy = jnp.clip(jax.random.uniform(key_of[7], (NOCC,), jnp.float32, -2.0, -0.5), -2.0, -0.5)
    return dict(half_integrals=half_integrals, domain_map=domain_map, domain_index=domain_index, owner_orbitals=owner_orbitals, pair_slots=pair_slots, pair_weight=pair_weight, virtual_energy=virtual_energy, occupied_energy=occupied_energy)


def transform_one(operands):
    integral, mapping, live_mask = operands
    product = jnp.dot(integral, mapping, preferred_element_type=jnp.float32)
    return (product * live_mask[None, :]).astype(jnp.bfloat16)


def reference(half_integrals, domain_map, domain_index, owner_orbitals, pair_slots, pair_weight, virtual_energy, occupied_energy):
    valid_slot = domain_index >= 0
    live_mask = valid_slot.astype(jnp.float32)
    domain_slabs = lax.map(transform_one, (half_integrals, domain_map, live_mask))
    safe_index = jnp.clip(domain_index, 0, NVIRT - 1).astype(jnp.int32)
    level = jnp.where(valid_slot, virtual_energy[safe_index], jnp.float32(1.0)).astype(jnp.float32)
    owner_of = (jnp.arange(NPAIRS) // PAIR_CAP).astype(jnp.int32)
    first_orb = owner_orbitals[owner_of, pair_slots[:, 0]].astype(jnp.int32)
    second_orb = owner_orbitals[owner_of, pair_slots[:, 1]].astype(jnp.int32)

    def one_pair(operands):
        left_orb, right_orb, weight_int = operands
        left_slab = domain_slabs[left_orb]
        right_slab = domain_slabs[right_orb]
        block = lax.dot_general(left_slab, right_slab, (((0,), (0,)), ((), ())), preferred_element_type=jnp.float32)
        denominator = level[left_orb][:, None] + level[right_orb][None, :] - occupied_energy[left_orb] - occupied_energy[right_orb]
        amp_ratio = block / denominator
        weight_float = weight_int.astype(jnp.float32)
        live_pair = (weight_int > 0).astype(jnp.float32)
        amplitude = (-amp_ratio * live_pair).astype(jnp.bfloat16)
        energy = -weight_float * jnp.sum(block * amp_ratio) / (DOM * DOM)
        squares = amp_ratio * amp_ratio
        row_grad = weight_float * jnp.sum(squares, axis=1) / DOM
        col_grad = weight_float * jnp.sum(squares, axis=0) / DOM
        return amplitude, energy, row_grad, col_grad

    amplitude, pair_energy, row_grad, col_grad = lax.map(one_pair, (first_orb, second_orb, pair_weight))
    domain_grad = jnp.zeros((NOCC, DOM), jnp.float32)
    domain_grad = domain_grad.at[first_orb].add(row_grad).at[second_orb].add(col_grad)
    return amplitude, pair_energy, domain_grad
```

```python
import jax
import jax.numpy as jnp
from jax import lax
from jax.experimental import pallas as pl
from jax.experimental.pallas import tpu as pltpu
from jax.sharding import PartitionSpec as P

F32 = jnp.float32
VMEM_LIMIT = 48 * 1024 * 1024
OWNERS_PER_STEP = 8
AUX_PER_STEP = 16


def slab_kernel(scalars, integral_ref, map_ref, index_ref, out_ref, slab_ref):
    occ_local = integral_ref.shape[0]
    per_step = out_ref.shape[0]
    step = pl.program_id(0)
    group = scalars[0]

    @pl.when(step == 0)
    def _():
        for orb in range(occ_local):
            product = jnp.dot(integral_ref[orb], map_ref[orb], preferred_element_type=F32)
            live = (index_ref[pl.ds(group * occ_local + orb, 1), :] >= 0).astype(F32)
            slab_ref[orb] = (product * live).astype(jnp.bfloat16)

    for k in range(per_step):
        out_ref[k] = slab_ref[scalars[1 + step * per_step + k]]


def make_slabs(half_integrals, domain_map, domain_index, own_local, orb_group):
    occ_local, rows, width = half_integrals.shape
    owners = own_local.shape[0]
    scalars = jnp.concatenate([orb_group[None].astype(jnp.int32), own_local])
    whole = lambda shape: pl.BlockSpec(shape, lambda i, s: (0,) * len(shape))
    return pl.pallas_call(
        slab_kernel,
        out_shape=jax.ShapeDtypeStruct((owners, rows, width), jnp.bfloat16),
        grid_spec=pltpu.PrefetchScalarGridSpec(
            num_scalar_prefetch=1,
            grid=(owners // OWNERS_PER_STEP,),
            in_specs=[
                whole(half_integrals.shape),
                whole(domain_map.shape),
                whole(domain_index.shape),
            ],
            out_specs=pl.BlockSpec((OWNERS_PER_STEP, rows, width), lambda i, s: (i, 0, 0)),
            scratch_shapes=[pltpu.VMEM((occ_local, rows, width), jnp.bfloat16)],
        ),
        compiler_params=pltpu.CompilerParams(vmem_limit_bytes=VMEM_LIMIT),
        name="slabs",
    )(scalars, half_integrals, domain_map, domain_index)


def gram_kernel(slots, slab_ref, out_ref, gram_ref):
    step = pl.program_id(0)
    count, list_width, rows, width = slab_ref.shape
    joined = jnp.concatenate(
        [slab_ref[:, g].reshape(count * rows, width) for g in range(list_width)], axis=1
    )
    part = lax.dot_general(joined, joined, (((0,), (0,)), ((), ())), preferred_element_type=F32)

    @pl.when(step == 0)
    def _():
        gram_ref[...] = part

    @pl.when(step > 0)
    def _():
        gram_ref[...] += part

    @pl.when(step == pl.num_programs(0) - 1)
    def _():
        for pair in range(out_ref.shape[0]):
            left = pl.multiple_of(slots[pair, 0] * width, width)
            right = pl.multiple_of(slots[pair, 1] * width, width)
            out_ref[pair] = gram_ref[pl.ds(left, width), pl.ds(right, width)]


def pair_blocks(slabs, pair_slots):
    aux, list_width, rows, width = slabs.shape
    pairs = pair_slots.shape[0]
    return pl.pallas_call(
        gram_kernel,
        out_shape=jax.ShapeDtypeStruct((pairs, width, width), F32),
        grid_spec=pltpu.PrefetchScalarGridSpec(
            num_scalar_prefetch=1,
            grid=(aux // AUX_PER_STEP,),
            in_specs=[
                pl.BlockSpec((AUX_PER_STEP, list_width, rows, width), lambda i, s: (i, 0, 0, 0))
            ],
            out_specs=pl.BlockSpec((pairs, width, width), lambda i, s: (0, 0, 0)),
            scratch_shapes=[pltpu.VMEM((list_width * width, list_width * width), F32)],
        ),
        compiler_params=pltpu.CompilerParams(vmem_limit_bytes=VMEM_LIMIT),
        name="pair_blocks",
    )(pair_slots, slabs)


def pair_kernel(slots, weights, occupied, first_pair, part_ref, level_ref, amp_ref, energy_ref, grad_ref, acc_ref):
    groups, share, width, _ = part_ref.shape
    list_width = level_ref.shape[0]
    acc_ref[...] = jnp.zeros_like(acc_ref)
    base = first_pair[0]
    for pair in range(share):
        left = slots[base + pair, 0]
        right = slots[base + pair, 1]
        weight_int = weights[base + pair]
        block = part_ref[0, pair]
        for g in range(1, groups):
            block = block + part_ref[g, pair]
        left_level = jnp.broadcast_to(level_ref[pl.ds(left, 1), :], (width, width)).T
        right_level = level_ref[pl.ds(right, 1), :]
        denominator = left_level + right_level - occupied[left] - occupied[right]
        ratio = block / denominator
        live = (weight_int > 0).astype(F32)
        weight = weight_int.astype(F32)
        amp_ref[pair] = (-ratio * live).astype(jnp.bfloat16)
        energy_ref[pair] = -weight * jnp.sum(block * ratio) / (width * width)
        squares = ratio * ratio
        scale = weight / width
        acc_ref[pl.ds(left, 1), :] += scale * jnp.sum(squares.T, axis=0, keepdims=True)
        acc_ref[pl.ds(right, 1), :] += scale * jnp.sum(squares, axis=0, keepdims=True)
    terms = acc_ref[...]
    for k in range(grad_ref.shape[0] // list_width):
        grad_ref[pl.ds(k * list_width, list_width), :] = terms


def pair_terms(parts, levels, pair_slots, pair_weight, occupied, first_pair, copies):
    groups, share, width, _ = parts.shape
    list_width = levels.shape[0]
    whole = pl.BlockSpec(memory_space=pltpu.VMEM)
    scalar = pl.BlockSpec(memory_space=pltpu.SMEM)
    return pl.pallas_call(
        pair_kernel,
        out_shape=(
            jax.ShapeDtypeStruct((share, width, width), jnp.bfloat16),
            jax.ShapeDtypeStruct((share,), F32),
            jax.ShapeDtypeStruct((copies * list_width, width), F32),
        ),
        in_specs=[scalar, scalar, scalar, scalar, whole, whole],
        out_specs=(whole, scalar, whole),
        scratch_shapes=[pltpu.VMEM((list_width, width), F32)],
        compiler_params=pltpu.CompilerParams(vmem_limit_bytes=VMEM_LIMIT),
        name="pair_terms",
    )(pair_slots, pair_weight, occupied, first_pair, parts, levels)


def grad_kernel(group, owner_ref, terms_ref, out_ref):
    occ_local, width = out_ref.shape
    owners = owner_ref.shape[1]
    per_owner = terms_ref.shape[0] // owners
    own = owner_ref[pl.ds(group[0], 1), :] - group[0] * occ_local
    chosen = (lax.broadcasted_iota(jnp.int32, (occ_local, owners), 0) == own).astype(F32)
    summed = jnp.sum(terms_ref[...].reshape(owners, per_owner, width), axis=1)
    out_ref[...] = jnp.dot(
        chosen, summed, preferred_element_type=F32, precision=lax.Precision.HIGHEST
    )


def sum_grads(terms, owner_orbitals, orb_group, occ_local):
    whole = pl.BlockSpec(memory_space=pltpu.VMEM)
    return pl.pallas_call(
        grad_kernel,
        out_shape=jax.ShapeDtypeStruct((occ_local, terms.shape[1]), F32),
        in_specs=[pl.BlockSpec(memory_space=pltpu.SMEM), whole, whole],
        out_specs=whole,
        compiler_params=pltpu.CompilerParams(vmem_limit_bytes=VMEM_LIMIT),
        name="sum_grads",
    )(orb_group[None].astype(jnp.int32), owner_orbitals.T, terms)


def on_device(
    half_integrals,
    domain_map,
    domain_index,
    owner_orbitals,
    pair_slots,
    pair_weight,
    virtual_energy,
    occupied_energy,
):
    orb_group = lax.axis_index("orb")
    owner_rank = lax.axis_index("aux")
    groups = lax.axis_size("orb")
    owners = lax.axis_size("aux")
    occ_local, rows, width = half_integrals.shape
    list_width = owner_orbitals.shape[1]
    share = pair_slots.shape[0] // groups

    own_local = (
        lax.dynamic_slice_in_dim(owner_orbitals, orb_group, 1, 1)[:, 0] - orb_group * occ_local
    )
    my_orbitals = lax.dynamic_slice_in_dim(owner_orbitals, owner_rank, 1, 0)[0]
    my_index = domain_index[my_orbitals]
    virt_count = virtual_energy.shape[0]
    levels = jnp.where(
        my_index >= 0, virtual_energy[jnp.clip(my_index, 0, virt_count - 1)], jnp.float32(1.0)
    )
    occupied = occupied_energy[my_orbitals]

    outgoing = make_slabs(half_integrals, domain_map, domain_index, own_local, orb_group)
    received = lax.all_to_all(
        outgoing.reshape(owners * groups, rows // groups, width),
        ("aux", "orb"),
        split_axis=0,
        concat_axis=0,
        tiled=True,
    )
    blocks = pair_blocks(
        received.reshape(owners, list_width, rows // groups, width), pair_slots
    )
    parts = lax.all_to_all(blocks, "orb", split_axis=0, concat_axis=0, tiled=True)
    amplitude, pair_energy, grad_terms = pair_terms(
        parts.reshape(groups, share, width, width),
        levels,
        pair_slots,
        pair_weight,
        occupied,
        (orb_group * share)[None].astype(jnp.int32),
        owners,
    )
    all_terms = lax.all_to_all(
        grad_terms, ("aux", "orb"), split_axis=0, concat_axis=0, tiled=True
    )
    domain_grad = sum_grads(all_terms, owner_orbitals, orb_group, occ_local)
    return (amplitude, pair_energy, domain_grad)


def solution(mesh):
    placed = (
        P("orb", "aux", None),
        P("orb", None, None),
        P(),
        P(),
        P("aux", None),
        P("aux"),
        P(),
        P(),
    )
    return jax.shard_map(
        on_device,
        mesh=mesh,
        in_specs=placed,
        out_specs=(P(("aux", "orb"), None, None), P(("aux", "orb")), P("orb", None)),
        check_vma=False,
    )
```

```python
import functools

import jax
import jax.numpy as jnp
from jax import lax
from jax.experimental import pallas as pl
from jax.experimental.pallas import tpu as pltpu
from jax.sharding import PartitionSpec as P

F32 = jnp.float32
VMEM_LIMIT = 48 * 1024 * 1024
OWNERS_PER_STEP = 8
AXES = ("zh", "zl", "yh", "yl", "c", "x")
BLOCKS = tuple((s, t) for s in range(4) for t in range(s, 4))
TAIL = 16
TOP_POWER = 14.0


def slab_kernel(scalars, integral_ref, map_ref, index_ref, out_ref, slab_ref):
    occ_local = integral_ref.shape[0]
    per_step = out_ref.shape[0]
    step = pl.program_id(0)
    group = scalars[0]

    @pl.when(step == 0)
    def _():
        for orb in range(occ_local):
            product = jnp.dot(integral_ref[orb], map_ref[orb], preferred_element_type=F32)
            live = (index_ref[pl.ds(group * occ_local + orb, 1), :] >= 0).astype(F32)
            slab_ref[orb] = (product * live).astype(jnp.bfloat16)

    for k in range(per_step):
        out_ref[k] = slab_ref[scalars[1 + step * per_step + k]]


def make_slabs(half_integrals, domain_map, domain_index, own_local, orb_group):
    occ_local, rows, width = half_integrals.shape
    owners = own_local.shape[0]
    scalars = jnp.concatenate([orb_group[None].astype(jnp.int32), own_local])
    whole = lambda shape: pl.BlockSpec(shape, lambda i, s: (0,) * len(shape))
    return pl.pallas_call(
        slab_kernel,
        out_shape=jax.ShapeDtypeStruct((owners, rows, width), jnp.bfloat16),
        grid_spec=pltpu.PrefetchScalarGridSpec(
            num_scalar_prefetch=1,
            grid=(owners // OWNERS_PER_STEP,),
            in_specs=[
                whole(half_integrals.shape),
                whole(domain_map.shape),
                whole(domain_index.shape),
            ],
            out_specs=pl.BlockSpec((OWNERS_PER_STEP, rows, width), lambda i, s: (i, 0, 0)),
            scratch_shapes=[pltpu.VMEM((occ_local, rows, width), jnp.bfloat16)],
        ),
        compiler_params=pltpu.CompilerParams(vmem_limit_bytes=VMEM_LIMIT),
        name="slabs",
    )(scalars, half_integrals, domain_map, domain_index)


def gram_kernel(slab_ref, out_ref, gram_ref):
    step = pl.program_id(1)
    count, list_width, _, rows, width = slab_ref.shape
    half = list_width * width // 2
    joined = jnp.concatenate(
        [slab_ref[:, g, 0].reshape(count * rows, width) for g in range(list_width)], axis=1
    )
    low, high = joined[:, :half], joined[:, half:]
    product = functools.partial(
        lax.dot_general,
        dimension_numbers=(((0,), (0,)), ((), ())),
        preferred_element_type=F32,
    )
    parts = (product(low, low), product(low, high), product(high, high))

    @pl.when(step == 0)
    def _():
        for k in range(3):
            gram_ref[k] = parts[k]

    @pl.when(step > 0)
    def _():
        for k in range(3):
            gram_ref[k] += parts[k]

    @pl.when(step == pl.num_programs(1) - 1)
    def _():
        top = jnp.max(jnp.max(jnp.abs(gram_ref[...]), axis=0), axis=0, keepdims=True)
        top = jnp.max(top, axis=1, keepdims=True)
        power = jnp.clip(jnp.ceil(jnp.log2(jnp.maximum(top, 1e-35))), -100.0, 100.0)
        power = jnp.broadcast_to(power, (8, width))
        scale = jnp.exp2(TOP_POWER - power)
        pieces = out_ref.shape[0]
        depth = width // pieces
        for index, (left, right) in enumerate(BLOCKS):
            quadrant = left // 2 + right // 2
            for q in range(pieces):
                row = (left % 2) * width + q * depth
                column = (right % 2) * width
                block = gram_ref[quadrant, row : row + depth, column : column + width]
                out_ref[q, 0, index * depth : (index + 1) * depth, :] = block * scale[0:1]
        for q in range(pieces):
            base = len(BLOCKS) * depth
            out_ref[q, 0, base : base + 8, :] = power
            out_ref[q, 0, base + 8 : base + TAIL, :] = power


def partial_grams(slabs):
    count, list_width, owners, rows, width = slabs.shape
    pieces = 4
    depth = len(BLOCKS) * (width // pieces) + TAIL
    steps = 2
    return pl.pallas_call(
        gram_kernel,
        out_shape=jax.ShapeDtypeStruct((pieces, owners, depth, width), F32),
        grid=(owners, steps),
        in_specs=[
            pl.BlockSpec(
                (count // steps, list_width, 1, rows, width), lambda j, h: (h, 0, j, 0, 0)
            )
        ],
        out_specs=pl.BlockSpec((pieces, 1, depth, width), lambda j, h: (0, j, 0, 0)),
        scratch_shapes=[pltpu.VMEM((3, list_width * width // 2, list_width * width // 2), F32)],
        compiler_params=pltpu.CompilerParams(vmem_limit_bytes=VMEM_LIMIT),
        name="partial_grams",
    )(slabs)


def pair_kernel(
    packed,
    occupied,
    piece_ref,
    block_ref,
    level_ref,
    amp0_ref,
    amp1_ref,
    amp2_ref,
    amp3_ref,
    grad_ref,
    ratio_ref,
    column_ref,
    place_ref,
    acc_ref,
    weight_table,
    energy_table,
):
    list_width, width = level_ref.shape
    depth = block_ref.shape[0] // len(BLOCKS)
    pairs = packed.shape[0]
    piece = piece_ref[0]
    rows = pl.ds(pl.multiple_of(piece * depth, depth), depth)
    for k in range(list_width * list_width):
        weight_table[k] = 0
    for pair in range(pairs):
        weight_table[packed[pair, 0] * list_width + packed[pair, 1]] = packed[pair, 2]
    for s in range(list_width):
        column_ref[s] = jnp.broadcast_to(level_ref[s : s + 1, :], (width, width)).T
    acc_ref[...] = jnp.zeros_like(acc_ref)
    place_ref[...] = jnp.zeros_like(place_ref)
    row_squares = [jnp.zeros((depth, width), F32) for _ in range(list_width)]
    for index, (left, right) in enumerate(BLOCKS):
        block = block_ref[index * depth : (index + 1) * depth, :]
        denominator = (
            column_ref[left, rows, :]
            + level_ref[right : right + 1, :]
            - occupied[left]
            - occupied[right]
        )
        ratio = block / denominator
        ratio_ref[index] = ratio
        energy_table[index] = jnp.sum(block * ratio)
        weight = weight_table[left * list_width + right]
        if left != right:
            weight = weight + weight_table[right * list_width + left]
        squares = (weight.astype(F32) / width) * (ratio * ratio)
        row_squares[left] = row_squares[left] + squares
        acc_ref[right : right + 1, :] += jnp.sum(squares, axis=0, keepdims=True)
    for s in range(list_width):
        place_ref[rows, :] = row_squares[s]
        acc_ref[s : s + 1, :] += jnp.sum(place_ref[...].T, axis=0, keepdims=True)

    def block_of(pair):
        low = jnp.minimum(packed[pair, 0], packed[pair, 1])
        high = jnp.maximum(packed[pair, 0], packed[pair, 1])
        return jnp.where(low == 0, 0, jnp.where(low == 1, 3, jnp.where(low == 2, 5, 6))) + high

    lane = lax.broadcasted_iota(jnp.int32, (1, width), 1)
    energies = jnp.zeros((1, width), F32)
    for pair in range(pairs):
        energy = -packed[pair, 2].astype(F32) * energy_table[block_of(pair)] / (width * width)
        energies = jnp.where(lane == pair, energy, energies)
    lines = []
    for s in range(list_width):
        lines.extend([acc_ref[s : s + 1, :], energies])
    tile = jnp.concatenate(lines, axis=0)
    height = tile.shape[0]
    for k in range(grad_ref.shape[0] // height):
        grad_ref[k * height : (k + 1) * height, :] = tile
    for shift, amp_ref in enumerate((amp0_ref, amp1_ref, amp2_ref, amp3_ref)):
        share = amp_ref.shape[0]
        quarter = jnp.bitwise_and(piece + shift, 3)
        for k in range(share):
            pair = quarter * share + k
            live = (packed[pair, 2] > 0).astype(F32)
            amp_ref[k] = (-ratio_ref[block_of(pair)] * live).astype(jnp.bfloat16)


def pair_terms(blocks, levels, packed, occupied, piece, copies):
    height, width = blocks.shape
    depth = height // len(BLOCKS)
    list_width = levels.shape[0]
    share = packed.shape[0] // 4
    whole = pl.BlockSpec(memory_space=pltpu.VMEM)
    scalar = pl.BlockSpec(memory_space=pltpu.SMEM)
    amp = jax.ShapeDtypeStruct((share, depth, width), jnp.bfloat16)
    return pl.pallas_call(
        pair_kernel,
        out_shape=(amp,) * 4
        + (jax.ShapeDtypeStruct((copies * 2 * list_width, width), F32),),
        in_specs=[scalar, scalar, scalar, whole, whole],
        out_specs=(whole,) * 5,
        scratch_shapes=[
            pltpu.VMEM((len(BLOCKS), depth, width), F32),
            pltpu.VMEM((list_width, width, width), F32),
            pltpu.VMEM((width, width), F32),
            pltpu.VMEM((list_width, width), F32),
            pltpu.SMEM((list_width * list_width,), jnp.int32),
            pltpu.SMEM((len(BLOCKS),), F32),
        ],
        compiler_params=pltpu.CompilerParams(vmem_limit_bytes=VMEM_LIMIT),
        name="pair_terms",
    )(packed, occupied, piece[None].astype(jnp.int32), blocks, levels)


def join_kernel(slots, quarter_ref, part0_ref, part1_ref, part2_ref, part3_ref, out_ref, place_ref):
    share, depth, width = part0_ref.shape
    quarter = quarter_ref[0]
    for k in range(share):
        for shift, part_ref in enumerate((part0_ref, part1_ref, part2_ref, part3_ref)):
            piece = jnp.bitwise_and(quarter + 4 - shift, 3)
            rows = pl.ds(pl.multiple_of(piece * depth, depth), depth)
            place_ref[rows, :] = part_ref[k].astype(F32)
        block = place_ref[...]
        pair = quarter * share + k
        swapped = slots[pair, 0] > slots[pair, 1]
        out_ref[k] = jnp.where(swapped, block.T, block).astype(jnp.bfloat16)


def join_amplitudes(parts, pair_slots, quarter):
    share, depth, width = parts[0].shape
    whole = pl.BlockSpec(memory_space=pltpu.VMEM)
    scalar = pl.BlockSpec(memory_space=pltpu.SMEM)
    return pl.pallas_call(
        join_kernel,
        out_shape=jax.ShapeDtypeStruct((share, width, width), jnp.bfloat16),
        in_specs=[scalar, scalar] + [whole] * 4,
        out_specs=whole,
        scratch_shapes=[pltpu.VMEM((width, width), F32)],
        compiler_params=pltpu.CompilerParams(vmem_limit_bytes=VMEM_LIMIT),
        name="join_amplitudes",
    )(pair_slots, quarter[None].astype(jnp.int32), *parts)


def grad_kernel(scalars, owner_ref, terms_ref, out_ref, energy_ref):
    occ_local, width = out_ref.shape
    lines = owner_ref.shape[1]
    share = energy_ref.shape[0]
    chosen = (
        lax.broadcasted_iota(jnp.int32, (occ_local, lines), 0) == owner_ref[...]
    ).astype(F32)
    out_ref[...] = jnp.dot(
        chosen, terms_ref[...], preferred_element_type=F32, precision=lax.Precision.HIGHEST
    )
    energies = terms_ref[pl.ds(scalars[1], 1), :]
    for k in range(2, scalars.shape[0]):
        energies = energies + terms_ref[pl.ds(scalars[k], 1), :]
    lane = lax.broadcasted_iota(jnp.int32, (1, width), 1)
    for k in range(share):
        energy_ref[k] = jnp.sum(jnp.where(lane == scalars[0] * share + k, energies, 0.0))


def sum_grads(terms, line_owner, scalars, occ_local, share):
    whole = pl.BlockSpec(memory_space=pltpu.VMEM)
    scalar = pl.BlockSpec(memory_space=pltpu.SMEM)
    return pl.pallas_call(
        grad_kernel,
        out_shape=(
            jax.ShapeDtypeStruct((occ_local, terms.shape[1]), F32),
            jax.ShapeDtypeStruct((share,), F32),
        ),
        in_specs=[scalar, whole, whole],
        out_specs=(whole, scalar),
        compiler_params=pltpu.CompilerParams(vmem_limit_bytes=VMEM_LIMIT),
        name="sum_grads",
    )(scalars, line_owner, terms)


def on_device(
    half_integrals,
    domain_map,
    domain_index,
    owner_orbitals,
    pair_slots,
    pair_weight,
    virtual_energy,
    occupied_energy,
):
    position = {name: lax.axis_index(name) for name in AXES}
    size = {name: lax.axis_size(name) for name in AXES}
    x = position["x"]

    def aux_rank(zh):
        rank = zh
        for name in AXES[1:-1]:
            rank = rank * size[name] + position[name]
        return rank

    occ_local, rows, width = half_integrals.shape
    owners, list_width = owner_orbitals.shape
    share = pair_slots.shape[0] // size["x"]
    cross = [(q * 4 + s, s * 4 + q) for q in range(4) for s in range(4)]

    packed = lax.ppermute(
        jnp.concatenate([pair_slots, pair_weight[:, None]], axis=1), ("zh", "x"), cross
    )
    own = lax.dynamic_slice_in_dim(owner_orbitals, x, 1, 1)[:, 0] - x * occ_local
    grid = own.reshape([size[name] for name in AXES[:-1]])
    order = grid.transpose(1, 3, 4, 0, 2).reshape(-1)
    source_own = jnp.broadcast_to(
        grid.transpose(1, 2, 3, 4, 0)[None], (size["zh"],) + grid.shape[1:] + grid.shape[:1]
    ).reshape(-1)
    line_owner = jnp.stack([source_own, jnp.full_like(source_own, -1)], axis=1).reshape(1, -1)

    my_orbitals = lax.dynamic_slice_in_dim(owner_orbitals, aux_rank(x), 1, 0)[0]
    my_index = domain_index[my_orbitals]
    virt_count = virtual_energy.shape[0]
    levels = jnp.where(
        my_index >= 0, virtual_energy[jnp.clip(my_index, 0, virt_count - 1)], jnp.float32(1.0)
    )
    occupied = occupied_energy[my_orbitals]

    outgoing = make_slabs(half_integrals, domain_map, domain_index, order, x)
    inner = ("zl", "yl", "c", "x")
    members = size["zl"] * size["yl"] * size["c"] * size["x"]
    per_member = owners // members
    received = lax.all_to_all(
        outgoing.reshape(members, per_member * rows, width),
        inner,
        split_axis=0,
        concat_axis=0,
        tiled=True,
    )
    scaled = partial_grams(
        received.reshape(members // size["x"], list_width, per_member, rows, width)
    )
    depth = scaled.shape[2]
    sent = scaled.astype(jnp.float16).reshape(-1, depth, width)
    arrived = lax.all_to_all(sent, ("zh", "yh"), split_axis=0, concat_axis=0, tiled=True)
    power = arrived[:, depth - TAIL : depth - TAIL + 1, :].astype(F32) - TOP_POWER
    blocks = jnp.sum(arrived[:, : depth - TAIL, :].astype(F32) * jnp.exp2(power), axis=0)

    *pieces, grad_terms = pair_terms(
        blocks, levels, packed, occupied, position["zh"], owners
    )
    moved = [
        lax.ppermute(
            piece,
            ("zh", "x"),
            [(q * 4 + s, s * 4 + (q + k) % 4) for q in range(4) for s in range(4)],
        )
        for k, piece in enumerate(pieces)
    ]
    all_terms = lax.all_to_all(grad_terms, AXES, split_axis=0, concat_axis=0, tiled=True)
    amplitude = join_amplitudes(moved, pair_slots, x)
    lines = [
        2 * (aux_rank(jnp.int32(q)) * size["x"] + position["zh"]) + 1 for q in range(size["zh"])
    ]
    scalars = jnp.stack([x] + lines).astype(jnp.int32)
    domain_grad, pair_energy = sum_grads(all_terms, line_owner, scalars, occ_local, share)
    return (amplitude, pair_energy, domain_grad)


def solution(mesh):
    fine = jax.sharding.Mesh(mesh.devices.reshape(4, 2, 4, 2, 2, 4), AXES)
    aux, orb = AXES[:-1], "x"
    placed = (
        P(orb, aux, None),
        P(orb, None, None),
        P(),
        P(),
        P(aux, None),
        P(aux),
        P(),
        P(),
    )
    return jax.shard_map(
        on_device,
        mesh=fine,
        in_specs=placed,
        out_specs=(P(AXES, None, None), P(AXES), P(orb, None)),
        check_vma=False,
    )
```

```python
import functools

import jax
import jax.numpy as jnp
from jax import lax
from jax.experimental import pallas as pl
from jax.experimental.pallas import tpu as pltpu
from jax.sharding import PartitionSpec as P

F32 = jnp.float32
VMEM_LIMIT = 48 * 1024 * 1024
SLAB_VMEM_LIMIT = 62 * 1024 * 1024
OWNERS_PER_STEP = 8
ORBS_PER_STEP = 8
AXES = ("zh", "zl", "yh", "yl", "c", "x")
BLOCKS = tuple((s, t) for s in range(4) for t in range(s, 4))
TAIL = 16
TOP_POWER = 14.0


def slab_kernel(scalars, integral_ref, map_ref, index_ref, out_ref, slab_ref):
    orbs = integral_ref.shape[0]
    per_step = out_ref.shape[0]
    step = pl.program_id(0)
    first_write = slab_ref.shape[0] // orbs

    @pl.when(step < first_write)
    def _():
        for k in range(orbs):
            orb = step * orbs + k
            live = index_ref[pl.ds(scalars[0] * slab_ref.shape[0] + orb, 1), :] >= 0
            masked = map_ref[k] * live.astype(F32).astype(jnp.bfloat16)
            slab_ref[orb] = lax.dot_general(
                masked.T, integral_ref[k], (((1,), (1,)), ((), ())), preferred_element_type=F32
            ).astype(jnp.bfloat16)

    @pl.when(step >= first_write)
    def _():
        for k in range(per_step):
            out_ref[k] = slab_ref[scalars[1 + (step - first_write) * per_step + k]]


def make_slabs(half_integrals, domain_map, domain_index, own_local, orb_group):
    occ_local, rows, width = half_integrals.shape
    owners = own_local.shape[0]
    scalars = jnp.concatenate([orb_group[None].astype(jnp.int32), own_local])
    parts = occ_local // ORBS_PER_STEP
    read = lambda i, s: (jnp.minimum(i, parts - 1), 0, 0)
    return pl.pallas_call(
        slab_kernel,
        out_shape=jax.ShapeDtypeStruct((owners, width, rows), jnp.bfloat16),
        grid_spec=pltpu.PrefetchScalarGridSpec(
            num_scalar_prefetch=1,
            grid=(parts + owners // OWNERS_PER_STEP,),
            in_specs=[
                pl.BlockSpec((ORBS_PER_STEP, rows, width), read),
                pl.BlockSpec((ORBS_PER_STEP, width, width), read),
                pl.BlockSpec(domain_index.shape, lambda i, s: (0, 0)),
            ],
            out_specs=pl.BlockSpec(
                (OWNERS_PER_STEP, width, rows), lambda i, s: (jnp.maximum(i - parts, 0), 0, 0)
            ),
            scratch_shapes=[pltpu.VMEM((occ_local, width, rows), jnp.bfloat16)],
        ),
        compiler_params=pltpu.CompilerParams(vmem_limit_bytes=SLAB_VMEM_LIMIT),
        name="slabs",
    )(scalars, half_integrals, domain_map, domain_index)


def gram_kernel(slab_ref, out_ref, gram_ref):
    step = pl.program_id(1)
    count, list_width, _, width, rows = slab_ref.shape
    half = list_width * width // 2
    middle = list_width // 2
    low = jnp.concatenate(
        [slab_ref[k, :middle, 0].reshape(half, rows) for k in range(count)], axis=1
    )
    high = jnp.concatenate(
        [slab_ref[k, middle:, 0].reshape(half, rows) for k in range(count)], axis=1
    )
    product = functools.partial(
        lax.dot_general,
        dimension_numbers=(((1,), (1,)), ((), ())),
        preferred_element_type=F32,
    )
    parts = (product(low, low), product(low, high), product(high, high))

    @pl.when(step == 0)
    def _():
        for k in range(3):
            gram_ref[k] = parts[k]

    @pl.when(step > 0)
    def _():
        for k in range(3):
            gram_ref[k] += parts[k]

    @pl.when(step == pl.num_programs(1) - 1)
    def _():
        top = jnp.max(jnp.max(jnp.abs(gram_ref[...]), axis=0), axis=0, keepdims=True)
        top = jnp.max(top, axis=1, keepdims=True)
        power = jnp.clip(jnp.ceil(jnp.log2(jnp.maximum(top, 1e-35))), -100.0, 100.0)
        power = jnp.broadcast_to(power, (8, width))
        scale = jnp.exp2(TOP_POWER - power)
        pieces = out_ref.shape[0]
        depth = width // pieces
        for index, (left, right) in enumerate(BLOCKS):
            quadrant = left // 2 + right // 2
            for q in range(pieces):
                row = (left % 2) * width + q * depth
                column = (right % 2) * width
                block = gram_ref[quadrant, row : row + depth, column : column + width]
                out_ref[q, 0, index * depth : (index + 1) * depth, :] = block * scale[0:1]
        for q in range(pieces):
            base = len(BLOCKS) * depth
            out_ref[q, 0, base : base + 8, :] = power
            out_ref[q, 0, base + 8 : base + TAIL, :] = power


def partial_grams(slabs):
    count, list_width, owners, width, rows = slabs.shape
    pieces = 4
    depth = len(BLOCKS) * (width // pieces) + TAIL
    steps = 2
    return pl.pallas_call(
        gram_kernel,
        out_shape=jax.ShapeDtypeStruct((pieces, owners, depth, width), F32),
        grid=(owners, steps),
        in_specs=[
            pl.BlockSpec(
                (count // steps, list_width, 1, width, rows), lambda j, h: (h, 0, j, 0, 0)
            )
        ],
        out_specs=pl.BlockSpec((pieces, 1, depth, width), lambda j, h: (0, j, 0, 0)),
        scratch_shapes=[pltpu.VMEM((3, list_width * width // 2, list_width * width // 2), F32)],
        compiler_params=pltpu.CompilerParams(vmem_limit_bytes=VMEM_LIMIT),
        name="partial_grams",
    )(slabs)


def split(value):
    high = value.astype(jnp.bfloat16).astype(F32)
    middle = (value - high).astype(jnp.bfloat16).astype(F32)
    return [high, middle, value - high - middle]


def pair_kernel(
    packed,
    occupied,
    place,
    block_ref,
    level_ref,
    out_ref,
    ratio_ref,
    column_ref,
    place_ref,
    acc_ref,
    weight_table,
    energy_table,
):
    list_width, width = level_ref.shape
    depth = block_ref.shape[0] // len(BLOCKS)
    pairs = packed.shape[0]
    piece, target = place[0], place[1]
    rows = pl.ds(pl.multiple_of(piece * depth, depth), depth)
    for k in range(list_width * list_width):
        weight_table[k] = 0
    for pair in range(pairs):
        weight_table[packed[pair, 0] * list_width + packed[pair, 1]] = packed[pair, 2]
    for s in range(list_width):
        column_ref[s] = jnp.broadcast_to(level_ref[s : s + 1, :], (width, width)).T
    acc_ref[...] = jnp.zeros_like(acc_ref)
    place_ref[...] = jnp.zeros_like(place_ref)
    row_squares = [jnp.zeros((depth, width), F32) for _ in range(list_width)]
    for index, (left, right) in enumerate(BLOCKS):
        block = block_ref[index * depth : (index + 1) * depth, :]
        denominator = (
            column_ref[left, rows, :]
            + level_ref[right : right + 1, :]
            - occupied[left]
            - occupied[right]
        )
        ratio = block / denominator
        ratio_ref[index] = ratio
        energy_table[index] = jnp.sum(block * ratio)
        weight = weight_table[left * list_width + right]
        if left != right:
            weight = weight + weight_table[right * list_width + left]
        squares = (weight.astype(F32) / width) * (ratio * ratio)
        row_squares[left] = row_squares[left] + squares
        acc_ref[right : right + 1, :] += jnp.sum(squares, axis=0, keepdims=True)
    for s in range(list_width):
        place_ref[rows, :] = row_squares[s]
        acc_ref[s : s + 1, :] += jnp.sum(place_ref[...].T, axis=0, keepdims=True)

    def block_of(pair):
        low = jnp.minimum(packed[pair, 0], packed[pair, 1])
        high = jnp.maximum(packed[pair, 0], packed[pair, 1])
        return jnp.where(low == 0, 0, jnp.where(low == 1, 3, jnp.where(low == 2, 5, 6))) + high

    lane = lax.broadcasted_iota(jnp.int32, (1, width), 1)
    energies = jnp.zeros((1, width), F32)
    for pair in range(pairs):
        energy = -packed[pair, 2].astype(F32) * energy_table[block_of(pair)] / (width * width)
        energies = jnp.where(lane == pair, energy, energies)
    share = pairs // list_width
    for quarter in range(list_width):
        lines = split(acc_ref[quarter : quarter + 1, :]) + split(energies)
        lines.append(jnp.zeros((TAIL - len(lines), width), F32))
        tail = jnp.concatenate(lines, axis=0).astype(jnp.bfloat16)
        for zone in range(out_ref.shape[0] // list_width):
            out_ref[zone * list_width + quarter, : share * depth, :] = jnp.zeros(
                (share * depth, width), jnp.bfloat16
            )
            out_ref[zone * list_width + quarter, share * depth :, :] = tail
    for pair in range(pairs):
        quarter, k = pair // share, pair % share
        live = (packed[pair, 2] > 0).astype(F32)
        value = (-ratio_ref[block_of(pair)] * live).astype(jnp.bfloat16)
        out_ref[target * list_width + quarter, k * depth : (k + 1) * depth, :] = value


def pair_terms(blocks, levels, packed, occupied, place):
    height, width = blocks.shape
    depth = height // len(BLOCKS)
    list_width = levels.shape[0]
    whole = pl.BlockSpec(memory_space=pltpu.VMEM)
    scalar = pl.BlockSpec(memory_space=pltpu.SMEM)
    rows = packed.shape[0] // list_width * depth + TAIL
    return pl.pallas_call(
        pair_kernel,
        out_shape=jax.ShapeDtypeStruct((4 * list_width, rows, width), jnp.bfloat16),
        in_specs=[scalar, scalar, scalar, whole, whole],
        out_specs=whole,
        scratch_shapes=[
            pltpu.VMEM((len(BLOCKS), depth, width), F32),
            pltpu.VMEM((list_width, width, width), F32),
            pltpu.VMEM((width, width), F32),
            pltpu.VMEM((list_width, width), F32),
            pltpu.SMEM((list_width * list_width,), jnp.int32),
            pltpu.SMEM((len(BLOCKS),), F32),
        ],
        compiler_params=pltpu.CompilerParams(vmem_limit_bytes=VMEM_LIMIT),
        name="pair_terms",
    )(packed, occupied, place, blocks, levels)


def owner_kernel(place, parts_ref, terms_ref, energy_ref):
    sources, height, width = parts_ref.shape
    zones = sources // 4
    share = energy_ref.shape[0]

    def tail(source):
        lines = parts_ref[source, height - TAIL :, :].astype(F32)
        return lines[0:1] + (lines[1:2] + lines[2:3]), lines[3:4] + (lines[4:5] + lines[5:6])

    vectors = []
    for s in range(4):
        vector = tail(s)[0]
        for q in range(1, zones):
            vector = vector + tail(q * 4 + s)[0]
        vectors.append(vector)
    tile = jnp.concatenate(vectors + vectors, axis=0)
    for k in range(terms_ref.shape[0] // 8):
        terms_ref[8 * k : 8 * k + 8, :] = tile
    energies = tail(place[0])[1]
    for q in range(1, zones):
        energies = energies + tail(q * 4 + place[0])[1]
    lane = lax.broadcasted_iota(jnp.int32, (1, width), 1)
    for k in range(share):
        energy_ref[k] = jnp.sum(jnp.where(lane == place[1] * share + k, energies, 0.0))


def owner_terms(parts, place, lines, share):
    whole = pl.BlockSpec(memory_space=pltpu.VMEM)
    scalar = pl.BlockSpec(memory_space=pltpu.SMEM)
    return pl.pallas_call(
        owner_kernel,
        out_shape=(
            jax.ShapeDtypeStruct((lines, parts.shape[2]), F32),
            jax.ShapeDtypeStruct((share,), F32),
        ),
        in_specs=[scalar, whole],
        out_specs=(whole, scalar),
        compiler_params=pltpu.CompilerParams(vmem_limit_bytes=VMEM_LIMIT),
        name="owner_terms",
    )(place, parts)


def join_kernel(slots, place, parts_ref, out_ref):
    share, width, _ = out_ref.shape
    sources, height, _ = parts_ref.shape
    depth = (height - TAIL) // share
    for k in range(share):
        block = jnp.concatenate(
            [
                parts_ref[q * 4 + place[0], k * depth : (k + 1) * depth, :].astype(F32)
                for q in range(sources // 4)
            ],
            axis=0,
        )
        pair = place[1] * share + k
        swapped = slots[pair, 0] > slots[pair, 1]
        out_ref[k] = jnp.where(swapped, block.T, block).astype(jnp.bfloat16)


def join_amplitudes(parts, pair_slots, place, share):
    whole = pl.BlockSpec(memory_space=pltpu.VMEM)
    scalar = pl.BlockSpec(memory_space=pltpu.SMEM)
    width = parts.shape[2]
    return pl.pallas_call(
        join_kernel,
        out_shape=jax.ShapeDtypeStruct((share, width, width), jnp.bfloat16),
        in_specs=[scalar, scalar, whole],
        out_specs=whole,
        compiler_params=pltpu.CompilerParams(vmem_limit_bytes=VMEM_LIMIT),
        name="join_amplitudes",
    )(pair_slots, place, parts)


def grad_kernel(owner_ref, terms_ref, out_ref):
    occ_local = out_ref.shape[0]
    lines = owner_ref.shape[1]
    chosen = (
        lax.broadcasted_iota(jnp.int32, (occ_local, lines), 0) == owner_ref[...]
    ).astype(F32)
    out_ref[...] = jnp.dot(
        chosen, terms_ref[...], preferred_element_type=F32, precision=lax.Precision.HIGHEST
    )


def sum_grads(terms, line_owner, occ_local):
    whole = pl.BlockSpec(memory_space=pltpu.VMEM)
    return pl.pallas_call(
        grad_kernel,
        out_shape=jax.ShapeDtypeStruct((occ_local, terms.shape[1]), F32),
        in_specs=[whole, whole],
        out_specs=whole,
        compiler_params=pltpu.CompilerParams(vmem_limit_bytes=VMEM_LIMIT),
        name="sum_grads",
    )(line_owner, terms)


def on_device(
    half_integrals,
    domain_map,
    domain_index,
    owner_orbitals,
    pair_slots,
    pair_weight,
    virtual_energy,
    occupied_energy,
):
    position = {name: lax.axis_index(name) for name in AXES}
    size = {name: lax.axis_size(name) for name in AXES}
    x = position["x"]

    def aux_rank(zh):
        rank = zh
        for name in AXES[1:-1]:
            rank = rank * size[name] + position[name]
        return rank

    occ_local, rows, width = half_integrals.shape
    owners, list_width = owner_orbitals.shape
    share = pair_slots.shape[0] // size["x"]
    cross = [(q * 4 + s, s * 4 + q) for q in range(4) for s in range(4)]

    packed = lax.ppermute(
        jnp.concatenate([pair_slots, pair_weight[:, None]], axis=1), ("zh", "x"), cross
    )
    own = lax.dynamic_slice_in_dim(owner_orbitals, x, 1, 1)[:, 0] - x * occ_local
    grid = own.reshape([size[name] for name in AXES[:-1]])
    order = grid.transpose(1, 3, 4, 0, 2).reshape(-1)
    line_owner = grid.transpose(1, 2, 3, 4, 0).reshape(1, -1)

    my_orbitals = lax.dynamic_slice_in_dim(owner_orbitals, aux_rank(x), 1, 0)[0]
    my_index = domain_index[my_orbitals]
    virt_count = virtual_energy.shape[0]
    levels = jnp.where(
        my_index >= 0, virtual_energy[jnp.clip(my_index, 0, virt_count - 1)], jnp.float32(1.0)
    )
    occupied = occupied_energy[my_orbitals]

    outgoing = make_slabs(half_integrals, domain_map, domain_index, order, x)
    inner = ("zl", "yl", "c", "x")
    members = size["zl"] * size["yl"] * size["c"] * size["x"]
    per_member = owners // members
    received = lax.all_to_all(
        outgoing.reshape(members, per_member * width, rows),
        inner,
        split_axis=0,
        concat_axis=0,
        tiled=True,
    )
    scaled = partial_grams(
        received.reshape(members // size["x"], list_width, per_member, width, rows)
    )
    depth = scaled.shape[2]
    sent = scaled.astype(jnp.float16).reshape(-1, depth, width)
    arrived = lax.all_to_all(sent, ("zh", "yh"), split_axis=0, concat_axis=0, tiled=True)
    power = arrived[:, depth - TAIL : depth - TAIL + 1, :].astype(F32) - TOP_POWER
    blocks = jnp.sum(arrived[:, : depth - TAIL, :].astype(F32) * jnp.exp2(power), axis=0)

    place = jnp.stack([position["zh"], x]).astype(jnp.int32)
    sent_terms = pair_terms(blocks, levels, packed, occupied, place)
    parts = lax.all_to_all(sent_terms, ("zh", "x"), split_axis=0, concat_axis=0, tiled=True)
    lines, pair_energy = owner_terms(parts, place, owners, share)
    all_lines = lax.all_to_all(
        lines, ("zl", "yh", "yl", "c"), split_axis=0, concat_axis=0, tiled=True
    )
    amplitude = join_amplitudes(parts, pair_slots, place, share)
    domain_grad = sum_grads(all_lines, line_owner, occ_local)
    return (amplitude, pair_energy, domain_grad)


def solution(mesh):
    fine = jax.sharding.Mesh(mesh.devices.reshape(4, 2, 4, 2, 2, 4), AXES)
    aux, orb = AXES[:-1], "x"
    placed = (
        P(orb, aux, None),
        P(orb, None, None),
        P(),
        P(),
        P(aux, None),
        P(aux),
        P(),
        P(),
    )
    return jax.shard_map(
        on_device,
        mesh=fine,
        in_specs=placed,
        out_specs=(P(AXES, None, None), P(AXES), P(orb, None)),
        check_vma=False,
    )
```

```python
import functools

import jax
import jax.numpy as jnp
from jax import lax
from jax.experimental import pallas as pl
from jax.experimental.pallas import tpu as pltpu
from jax.sharding import PartitionSpec as P

F32 = jnp.float32
VMEM_LIMIT = 48 * 1024 * 1024
SLAB_VMEM_LIMIT = 62 * 1024 * 1024
OWNERS_PER_STEP = 32
ORBS_PER_STEP = 16
GRAMS_PER_STEP = 2
AXES = ("zh", "zl", "yh", "yl", "c", "x")
BLOCKS = tuple((s, t) for s in range(4) for t in range(s, 4))
TAIL = 16
TOP_POWER = 14.0


def slab_kernel(owner_list, group, integral_ref, map_ref, index_ref, out_ref, slab_ref):
    orbs = integral_ref.shape[0]
    occ_local = slab_ref.shape[0]
    per_step = out_ref.shape[0]
    step = pl.program_id(0)
    first_write = occ_local // orbs
    first_orb = group[0] * occ_local

    @pl.when(step < first_write)
    def _():
        for k in range(orbs):
            orb = step * orbs + k
            live = index_ref[pl.ds(first_orb + orb, 1), :] >= 0
            masked = map_ref[k] * live.astype(F32).astype(jnp.bfloat16)
            slab_ref[orb] = lax.dot_general(
                masked.T, integral_ref[k], (((1,), (1,)), ((), ())), preferred_element_type=F32
            ).astype(jnp.bfloat16)

    @pl.when(step >= first_write)
    def _():
        part = step - first_write
        base = jnp.right_shift(part, 1) * 16 + jnp.bitwise_and(part, 1) * 2
        for k in range(per_step):
            owner = base + (k // 4 % 4) * 32 + (k % 4) * 4 + k // 16
            out_ref[k] = slab_ref[owner_list[group[0], owner] - first_orb]


def make_slabs(half_integrals, domain_map, domain_index, owner_orbitals, orb_group):
    occ_local, rows, width = half_integrals.shape
    owners = owner_orbitals.shape[0]
    parts = occ_local // ORBS_PER_STEP
    read = lambda i, s, t: (jnp.minimum(i, parts - 1), 0, 0)
    return pl.pallas_call(
        slab_kernel,
        out_shape=jax.ShapeDtypeStruct((owners, width, rows), jnp.bfloat16),
        grid_spec=pltpu.PrefetchScalarGridSpec(
            num_scalar_prefetch=2,
            grid=(parts + owners // OWNERS_PER_STEP,),
            in_specs=[
                pl.BlockSpec((ORBS_PER_STEP, rows, width), read),
                pl.BlockSpec((ORBS_PER_STEP, width, width), read),
                pl.BlockSpec(domain_index.shape, lambda i, s, t: (0, 0)),
            ],
            out_specs=pl.BlockSpec(
                (OWNERS_PER_STEP, width, rows), lambda i, s, t: (jnp.maximum(i - parts, 0), 0, 0)
            ),
            scratch_shapes=[pltpu.VMEM((occ_local, width, rows), jnp.bfloat16)],
        ),
        compiler_params=pltpu.CompilerParams(vmem_limit_bytes=SLAB_VMEM_LIMIT),
        name="slabs",
    )(
        owner_orbitals.T,
        orb_group[None].astype(jnp.int32),
        half_integrals,
        domain_map,
        domain_index,
    )


def gram_kernel(slab_ref, out_ref):
    count, list_width, owners, width, rows = slab_ref.shape
    half = list_width * width // 2
    middle = list_width // 2
    product = functools.partial(
        lax.dot_general,
        dimension_numbers=(((1,), (1,)), ((), ())),
        preferred_element_type=F32,
    )
    pieces = out_ref.shape[0]
    depth = width // pieces
    base = len(BLOCKS) * depth
    for j in range(owners):
        low = jnp.concatenate(
            [slab_ref[k, :middle, j].reshape(half, rows) for k in range(count)], axis=1
        )
        high = jnp.concatenate(
            [slab_ref[k, middle:, j].reshape(half, rows) for k in range(count)], axis=1
        )
        parts = (product(low, low), product(low, high), product(high, high))

        def block_at(left, right):
            row, column = left % 2 * width, right % 2 * width
            return parts[left // 2 + right // 2][row : row + width, column : column + width]

        top = jnp.zeros((8, width), F32)
        for s in range(list_width):
            top = jnp.maximum(
                top, jnp.max(jnp.abs(block_at(s, s)).reshape(width // 8, 8, width), axis=0)
            )
        top = jnp.max(jnp.max(top, axis=0, keepdims=True), axis=1, keepdims=True)
        power = jnp.clip(jnp.ceil(jnp.log2(jnp.maximum(top, 1e-35))), -100.0, 100.0)
        power = jnp.broadcast_to(power, (8, width))
        scale = jnp.exp2(TOP_POWER - power)[0:1]
        for index, (left, right) in enumerate(BLOCKS):
            block = block_at(left, right) * scale
            for q in range(pieces):
                out_ref[q, j, index * depth : (index + 1) * depth, :] = block[
                    q * depth : (q + 1) * depth
                ]
        for q in range(pieces):
            out_ref[q, j, base : base + 8, :] = power
            out_ref[q, j, base + 8 : base + TAIL, :] = power


def partial_grams(slabs):
    count, list_width, owners, width, rows = slabs.shape
    pieces = 4
    depth = len(BLOCKS) * (width // pieces) + TAIL
    return pl.pallas_call(
        gram_kernel,
        out_shape=jax.ShapeDtypeStruct((pieces, owners, depth, width), F32),
        grid=(owners // GRAMS_PER_STEP,),
        in_specs=[
            pl.BlockSpec(
                (count, list_width, GRAMS_PER_STEP, width, rows), lambda j: (0, 0, j, 0, 0)
            )
        ],
        out_specs=pl.BlockSpec((pieces, GRAMS_PER_STEP, depth, width), lambda j: (0, j, 0, 0)),
        compiler_params=pltpu.CompilerParams(vmem_limit_bytes=VMEM_LIMIT),
        name="partial_grams",
    )(slabs)


def split(value):
    high = value.astype(jnp.bfloat16).astype(F32)
    middle = (value - high).astype(jnp.bfloat16).astype(F32)
    return [high, middle, value - high - middle]


def pair_kernel(
    packed,
    occupied,
    place,
    block_ref,
    level_ref,
    out_ref,
    ratio_ref,
    column_ref,
    place_ref,
    acc_ref,
    weight_table,
    energy_table,
):
    list_width, width = level_ref.shape
    depth = block_ref.shape[0] // len(BLOCKS)
    pairs = packed.shape[0]
    piece = place[0]
    rows = pl.ds(pl.multiple_of(piece * depth, depth), depth)
    for k in range(list_width * list_width):
        weight_table[k] = 0
    for pair in range(pairs):
        weight_table[packed[pair, 0] * list_width + packed[pair, 1]] = packed[pair, 2]
    for s in range(list_width):
        column_ref[s] = jnp.broadcast_to(level_ref[s : s + 1, :], (width, width)).T
    acc_ref[...] = jnp.zeros_like(acc_ref)
    place_ref[...] = jnp.zeros_like(place_ref)
    row_squares = [jnp.zeros((depth, width), F32) for _ in range(list_width)]
    for index, (left, right) in enumerate(BLOCKS):
        block = block_ref[index * depth : (index + 1) * depth, :]
        denominator = (
            column_ref[left, rows, :]
            + level_ref[right : right + 1, :]
            - occupied[left]
            - occupied[right]
        )
        ratio = block / denominator
        ratio_ref[index] = ratio
        energy_table[index] = jnp.sum(block * ratio)
        weight = weight_table[left * list_width + right]
        if left != right:
            weight = weight + weight_table[right * list_width + left]
        squares = (weight.astype(F32) / width) * (ratio * ratio)
        row_squares[left] = row_squares[left] + squares
        acc_ref[right : right + 1, :] += jnp.sum(squares, axis=0, keepdims=True)
    for s in range(list_width):
        place_ref[rows, :] = row_squares[s]
        acc_ref[s : s + 1, :] += jnp.sum(place_ref[...].T, axis=0, keepdims=True)

    def block_of(pair):
        low = jnp.minimum(packed[pair, 0], packed[pair, 1])
        high = jnp.maximum(packed[pair, 0], packed[pair, 1])
        return jnp.where(low == 0, 0, jnp.where(low == 1, 3, jnp.where(low == 2, 5, 6))) + high

    lane = lax.broadcasted_iota(jnp.int32, (1, width), 1)
    energies = jnp.zeros((1, width), F32)
    for pair in range(pairs):
        energy = -packed[pair, 2].astype(F32) * energy_table[block_of(pair)] / (width * width)
        energies = jnp.where(lane == pair, energy, energies)
    share = pairs // list_width
    for quarter in range(list_width):
        lines = split(acc_ref[quarter : quarter + 1, :]) + split(energies)
        lines.append(jnp.zeros((TAIL - len(lines), width), F32))
        tail = jnp.concatenate(lines, axis=0).astype(jnp.bfloat16)
        out_ref[quarter, share * depth :, :] = tail
    for pair in range(pairs):
        quarter, k = pair // share, pair % share
        live = (packed[pair, 2] > 0).astype(F32)
        value = (-ratio_ref[block_of(pair)] * live).astype(jnp.bfloat16)
        out_ref[quarter, k * depth : (k + 1) * depth, :] = value


def pair_terms(blocks, levels, packed, occupied, place):
    height, width = blocks.shape
    depth = height // len(BLOCKS)
    list_width = levels.shape[0]
    whole = pl.BlockSpec(memory_space=pltpu.VMEM)
    scalar = pl.BlockSpec(memory_space=pltpu.SMEM)
    rows = packed.shape[0] // list_width * depth + TAIL
    return pl.pallas_call(
        pair_kernel,
        out_shape=jax.ShapeDtypeStruct((list_width, rows, width), jnp.bfloat16),
        in_specs=[scalar, scalar, scalar, whole, whole],
        out_specs=whole,
        scratch_shapes=[
            pltpu.VMEM((len(BLOCKS), depth, width), F32),
            pltpu.VMEM((list_width, width, width), F32),
            pltpu.VMEM((width, width), F32),
            pltpu.VMEM((list_width, width), F32),
            pltpu.SMEM((list_width * list_width,), jnp.int32),
            pltpu.SMEM((len(BLOCKS),), F32),
        ],
        compiler_params=pltpu.CompilerParams(vmem_limit_bytes=VMEM_LIMIT),
        name="pair_terms",
    )(packed, occupied, place, blocks, levels)


def plane_kernel(parts_ref, out_ref):
    owners, height, width = parts_ref.shape
    body = height - TAIL
    tails = [parts_ref[s, body:, :].astype(F32) for s in range(owners)]
    vectors = [tails[s][k : k + 1] for k in range(3) for s in range(owners)]
    per_zone = out_ref.shape[0] // owners
    for s in range(owners):
        lines = vectors + [tails[s][3:6], jnp.zeros((TAIL - 3 * owners - 3, width), F32)]
        tail = jnp.concatenate(lines, axis=0).astype(jnp.bfloat16)
        for k in range(per_zone):
            out_ref[s * per_zone + k, :body, :] = parts_ref[s, :body, :]
            out_ref[s * per_zone + k, body:, :] = tail


def plane_terms(parts, planes):
    whole = pl.BlockSpec(memory_space=pltpu.VMEM)
    return pl.pallas_call(
        plane_kernel,
        out_shape=jax.ShapeDtypeStruct((planes,) + parts.shape[1:], parts.dtype),
        in_specs=[whole],
        out_specs=whole,
        compiler_params=pltpu.CompilerParams(vmem_limit_bytes=VMEM_LIMIT),
        name="plane_terms",
    )(parts)


def owner_kernel(place, parts_ref, terms_ref, energy_ref):
    planes, height, width = parts_ref.shape
    share = energy_ref.shape[0]
    body = height - TAIL
    sums = []
    for low in range(2):
        total = None
        for q in range(planes // 2):
            tail = parts_ref[q * 2 + low, body:, :].astype(F32)
            vectors = tail[0:4] + (tail[4:8] + tail[8:12])
            total = vectors if total is None else total + vectors
        sums.append(total)
    tile = jnp.concatenate(sums, axis=0)
    for k in range(terms_ref.shape[0] // 8):
        terms_ref[8 * k : 8 * k + 8, :] = tile
    energies = jnp.zeros((1, width), F32)
    for q in range(planes // 2):
        tail = parts_ref[q * 2 + place[1], body:, :].astype(F32)
        energies = energies + (tail[12:13] + (tail[13:14] + tail[14:15]))
    lane = lax.broadcasted_iota(jnp.int32, (1, width), 1)
    for k in range(share):
        energy_ref[k] = jnp.sum(jnp.where(lane == place[2] * share + k, energies, 0.0))


def owner_terms(parts, place, lines, share):
    whole = pl.BlockSpec(memory_space=pltpu.VMEM)
    scalar = pl.BlockSpec(memory_space=pltpu.SMEM)
    return pl.pallas_call(
        owner_kernel,
        out_shape=(
            jax.ShapeDtypeStruct((lines, parts.shape[2]), F32),
            jax.ShapeDtypeStruct((share,), F32),
        ),
        in_specs=[scalar, whole],
        out_specs=(whole, scalar),
        compiler_params=pltpu.CompilerParams(vmem_limit_bytes=VMEM_LIMIT),
        name="owner_terms",
    )(place, parts)


def join_kernel(slots, place, parts_ref, out_ref):
    share, width, _ = out_ref.shape
    sources, height, _ = parts_ref.shape
    depth = (height - TAIL) // share
    for k in range(share):
        block = jnp.concatenate(
            [
                parts_ref[q * 2 + place[1], k * depth : (k + 1) * depth, :].astype(F32)
                for q in range(sources // 2)
            ],
            axis=0,
        )
        pair = place[2] * share + k
        swapped = slots[pair, 0] > slots[pair, 1]
        out_ref[k] = jnp.where(swapped, block.T, block).astype(jnp.bfloat16)


def join_amplitudes(parts, pair_slots, place, share):
    whole = pl.BlockSpec(memory_space=pltpu.VMEM)
    scalar = pl.BlockSpec(memory_space=pltpu.SMEM)
    width = parts.shape[2]
    return pl.pallas_call(
        join_kernel,
        out_shape=jax.ShapeDtypeStruct((share, width, width), jnp.bfloat16),
        in_specs=[scalar, scalar, whole],
        out_specs=whole,
        compiler_params=pltpu.CompilerParams(vmem_limit_bytes=VMEM_LIMIT),
        name="join_amplitudes",
    )(pair_slots, place, parts)


def grad_kernel(owner_ref, terms_ref, out_ref):
    occ_local = out_ref.shape[0]
    lines = owner_ref.shape[1]
    chosen = (
        lax.broadcasted_iota(jnp.int32, (occ_local, lines), 0) == owner_ref[...]
    ).astype(F32)
    out_ref[...] = jnp.dot(
        chosen, terms_ref[...], preferred_element_type=F32, precision=lax.Precision.HIGHEST
    )


def sum_grads(terms, line_owner, occ_local):
    whole = pl.BlockSpec(memory_space=pltpu.VMEM)
    return pl.pallas_call(
        grad_kernel,
        out_shape=jax.ShapeDtypeStruct((occ_local, terms.shape[1]), F32),
        in_specs=[whole, whole],
        out_specs=whole,
        compiler_params=pltpu.CompilerParams(vmem_limit_bytes=VMEM_LIMIT),
        name="sum_grads",
    )(line_owner, terms)


def on_device(
    half_integrals,
    domain_map,
    domain_index,
    owner_orbitals,
    pair_slots,
    pair_weight,
    virtual_energy,
    occupied_energy,
):
    position = {name: lax.axis_index(name) for name in AXES}
    size = {name: lax.axis_size(name) for name in AXES}
    x = position["x"]

    def aux_rank(zh):
        rank = zh
        for name in AXES[1:-1]:
            rank = rank * size[name] + position[name]
        return rank

    occ_local, rows, width = half_integrals.shape
    owners, list_width = owner_orbitals.shape
    share = pair_slots.shape[0] // size["x"]
    cross = [(q * 4 + s, s * 4 + q) for q in range(4) for s in range(4)]

    packed = lax.ppermute(
        jnp.concatenate([pair_slots, pair_weight[:, None]], axis=1), ("zh", "x"), cross
    )
    own = lax.dynamic_slice_in_dim(owner_orbitals, x, 1, 1)[:, 0] - x * occ_local
    grid = own.reshape([size[name] for name in AXES[:-1]])
    line_owner = grid.transpose(2, 3, 4, 1, 0).reshape(1, -1)

    my_orbitals = lax.dynamic_slice_in_dim(owner_orbitals, aux_rank(x), 1, 0)[0]
    my_index = domain_index[my_orbitals]
    virt_count = virtual_energy.shape[0]
    levels = jnp.where(
        my_index >= 0, virtual_energy[jnp.clip(my_index, 0, virt_count - 1)], jnp.float32(1.0)
    )
    occupied = occupied_energy[my_orbitals]

    outgoing = make_slabs(half_integrals, domain_map, domain_index, owner_orbitals, x)
    inner = ("zl", "yl", "c", "x")
    members = size["zl"] * size["yl"] * size["c"] * size["x"]
    per_member = owners // members
    received = lax.all_to_all(
        outgoing.reshape(members, per_member * width, rows),
        inner,
        split_axis=0,
        concat_axis=0,
        tiled=True,
    )
    scaled = partial_grams(
        received.reshape(members // size["x"], list_width, per_member, width, rows)
    )
    depth = scaled.shape[2]
    sent = scaled.astype(jnp.float16).reshape(-1, depth, width)
    arrived = lax.all_to_all(sent, ("zh", "yh"), split_axis=0, concat_axis=0, tiled=True)
    power = arrived[:, depth - TAIL : depth - TAIL + 1, :].astype(F32) - TOP_POWER
    blocks = jnp.sum(arrived[:, : depth - TAIL, :].astype(F32) * jnp.exp2(power), axis=0)

    place = jnp.stack([position["zh"], position["zl"], x]).astype(jnp.int32)
    slices = pair_terms(blocks, levels, packed, occupied, place)
    slices = lax.all_to_all(slices, "x", split_axis=0, concat_axis=0, tiled=True)
    planes = plane_terms(slices, size["zh"] * size["zl"])
    parts = lax.all_to_all(planes, ("zh", "zl"), split_axis=0, concat_axis=0, tiled=True)
    lines, pair_energy = owner_terms(parts, place, owners, share)
    all_lines = lax.all_to_all(lines, ("yh", "yl", "c"), split_axis=0, concat_axis=0, tiled=True)
    amplitude = join_amplitudes(parts, pair_slots, place, share)
    domain_grad = sum_grads(all_lines, line_owner, occ_local)
    return (amplitude, pair_energy, domain_grad)


def solution(mesh):
    fine = jax.sharding.Mesh(mesh.devices.reshape(4, 2, 4, 2, 2, 4), AXES)
    aux, orb = AXES[:-1], "x"
    placed = (
        P(orb, aux, None),
        P(orb, None, None),
        P(),
        P(),
        P(aux, None),
        P(aux),
        P(),
        P(),
    )
    return jax.shard_map(
        on_device,
        mesh=fine,
        in_specs=placed,
        out_specs=(P(AXES, None, None), P(AXES), P(orb, None)),
        check_vma=False,
    )
```

```python
import functools

import jax
import jax.numpy as jnp
from jax import lax
from jax.experimental import pallas as pl
from jax.experimental.pallas import tpu as pltpu
from jax.sharding import PartitionSpec as P

F32 = jnp.float32
VMEM_LIMIT = 48 * 1024 * 1024
SLAB_VMEM_LIMIT = 62 * 1024 * 1024
OWNERS_PER_STEP = 32
ORBS_PER_STEP = 16
GRAMS_PER_STEP = 2
AXES = ("zh", "zl", "yh", "yl", "c", "x")
BLOCKS = tuple((s, t) for s in range(4) for t in range(s, 4))
CROSS = tuple((s, t) for s, t in BLOCKS if s < t)
SENT = len(CROSS) + 2
TAIL = 16
TOP_POWER = 14.0


def slab_kernel(owner_list, group, integral_ref, map_ref, index_ref, out_ref, slab_ref):
    orbs = integral_ref.shape[0]
    occ_local = slab_ref.shape[0]
    per_step = out_ref.shape[0]
    step = pl.program_id(0)
    first_write = occ_local // orbs
    first_orb = group[0] * occ_local

    @pl.when(step < first_write)
    def _():
        for k in range(orbs):
            orb = step * orbs + k
            live = index_ref[pl.ds(first_orb + orb, 1), :] >= 0
            masked = map_ref[k] * live.astype(F32).astype(jnp.bfloat16)
            slab_ref[orb] = lax.dot_general(
                masked.T, integral_ref[k], (((1,), (1,)), ((), ())), preferred_element_type=F32
            ).astype(jnp.bfloat16)

    @pl.when(step >= first_write)
    def _():
        part = step - first_write
        base = jnp.right_shift(part, 1) * 16 + jnp.bitwise_and(part, 1) * 2
        for k in range(per_step):
            owner = base + (k // 4 % 4) * 32 + (k % 4) * 4 + k // 16
            out_ref[k] = slab_ref[owner_list[group[0], owner] - first_orb]


def make_slabs(half_integrals, domain_map, domain_index, owner_orbitals, orb_group):
    occ_local, rows, width = half_integrals.shape
    owners = owner_orbitals.shape[0]
    parts = occ_local // ORBS_PER_STEP
    read = lambda i, s, t: (jnp.minimum(i, parts - 1), 0, 0)
    return pl.pallas_call(
        slab_kernel,
        out_shape=jax.ShapeDtypeStruct((owners, width, rows), jnp.bfloat16),
        grid_spec=pltpu.PrefetchScalarGridSpec(
            num_scalar_prefetch=2,
            grid=(parts + owners // OWNERS_PER_STEP,),
            in_specs=[
                pl.BlockSpec((ORBS_PER_STEP, rows, width), read),
                pl.BlockSpec((ORBS_PER_STEP, width, width), read),
                pl.BlockSpec(domain_index.shape, lambda i, s, t: (0, 0)),
            ],
            out_specs=pl.BlockSpec(
                (OWNERS_PER_STEP, width, rows), lambda i, s, t: (jnp.maximum(i - parts, 0), 0, 0)
            ),
            scratch_shapes=[pltpu.VMEM((occ_local, width, rows), jnp.bfloat16)],
        ),
        compiler_params=pltpu.CompilerParams(vmem_limit_bytes=SLAB_VMEM_LIMIT),
        name="slabs",
    )(
        owner_orbitals.T,
        orb_group[None].astype(jnp.int32),
        half_integrals,
        domain_map,
        domain_index,
    )


def gram_kernel(slab_ref, out_ref):
    count, list_width, owners, width, rows = slab_ref.shape
    half = list_width * width // 2
    middle = list_width // 2
    product = functools.partial(
        lax.dot_general,
        dimension_numbers=(((1,), (1,)), ((), ())),
        preferred_element_type=F32,
    )
    pieces = out_ref.shape[0]
    depth = width // pieces
    base = SENT * depth
    line = lax.broadcasted_iota(jnp.int32, (width, width), 0)
    lane = lax.broadcasted_iota(jnp.int32, (width, width), 1)
    for j in range(owners):
        low = jnp.concatenate(
            [slab_ref[k, :middle, j].reshape(half, rows) for k in range(count)], axis=1
        )
        high = jnp.concatenate(
            [slab_ref[k, middle:, j].reshape(half, rows) for k in range(count)], axis=1
        )
        parts = (product(low, low), product(low, high), product(high, high))

        def block_at(left, right):
            row, column = left % 2 * width, right % 2 * width
            return parts[left // 2 + right // 2][row : row + width, column : column + width]

        top = jnp.zeros((8, width), F32)
        for s in range(list_width):
            top = jnp.maximum(
                top, jnp.max(jnp.abs(block_at(s, s)).reshape(width // 8, 8, width), axis=0)
            )
        top = jnp.max(jnp.max(top, axis=0, keepdims=True), axis=1, keepdims=True)
        power = jnp.clip(jnp.ceil(jnp.log2(jnp.maximum(top, 1e-35))), -100.0, 100.0)
        power = jnp.broadcast_to(power, (8, width))
        scale = jnp.exp2(TOP_POWER - power)[0:1]
        blocks = [block_at(left, right) for left, right in CROSS]
        diagonals = []
        for s in range(0, list_width, 2):
            lower = block_at(s + 1, s + 1)
            blocks.append(jnp.where(lane >= line, block_at(s, s), lower))
            diagonals.append(
                jnp.sum(jnp.where(lane == line, lower, 0.0), axis=0, keepdims=True) * scale
            )
        tail = jnp.concatenate(diagonals + [power[: 8 - len(diagonals)]], axis=0)
        for index, block in enumerate(blocks):
            block = block * scale
            for q in range(pieces):
                out_ref[q, j, index * depth : (index + 1) * depth, :] = block[
                    q * depth : (q + 1) * depth
                ]
        for q in range(pieces):
            out_ref[q, j, base : base + 8, :] = tail
            out_ref[q, j, base + 8 : base + TAIL, :] = power


def partial_grams(slabs):
    count, list_width, owners, width, rows = slabs.shape
    pieces = 4
    depth = SENT * (width // pieces) + TAIL
    return pl.pallas_call(
        gram_kernel,
        out_shape=jax.ShapeDtypeStruct((pieces, owners, depth, width), F32),
        grid=(owners // GRAMS_PER_STEP,),
        in_specs=[
            pl.BlockSpec(
                (count, list_width, GRAMS_PER_STEP, width, rows), lambda j: (0, 0, j, 0, 0)
            )
        ],
        out_specs=pl.BlockSpec((pieces, GRAMS_PER_STEP, depth, width), lambda j: (0, j, 0, 0)),
        compiler_params=pltpu.CompilerParams(vmem_limit_bytes=VMEM_LIMIT),
        name="partial_grams",
    )(slabs)


def split(value):
    high = value.astype(jnp.bfloat16).astype(F32)
    middle = (value - high).astype(jnp.bfloat16).astype(F32)
    return [high, middle, value - high - middle]


def pair_kernel(
    packed,
    occupied,
    place,
    block_ref,
    level_ref,
    out_ref,
    ratio_ref,
    column_ref,
    place_ref,
    acc_ref,
    weight_table,
    energy_table,
):
    list_width, width = level_ref.shape
    depth = (block_ref.shape[0] - 8) // SENT
    pairs = packed.shape[0]
    piece = place[0]
    rows = pl.ds(pl.multiple_of(piece * depth, depth), depth)
    for k in range(list_width * list_width):
        weight_table[k] = 0
    for pair in range(pairs):
        weight_table[packed[pair, 0] * list_width + packed[pair, 1]] = packed[pair, 2]
    for s in range(list_width):
        column_ref[s] = jnp.broadcast_to(level_ref[s : s + 1, :], (width, width)).T
    acc_ref[...] = jnp.zeros_like(acc_ref)
    place_ref[...] = jnp.zeros_like(place_ref)
    row_squares = [jnp.zeros((depth, width), F32) for _ in range(list_width)]
    line = lax.broadcasted_iota(jnp.int32, (depth, width), 0) + piece * depth
    column = lax.broadcasted_iota(jnp.int32, (depth, width), 1)

    def block_at(index):
        return block_ref[index * depth : (index + 1) * depth, :]

    for index, (left, right) in enumerate(BLOCKS):
        if left != right:
            block = block_at(CROSS.index((left, right)))
        else:
            block = block_at(len(CROSS) + left // 2)
            if left % 2 == 0:
                block = jnp.where(column >= line, block, 0.0)
            else:
                row = SENT * depth + left // 2
                inner = jnp.where(column == line, block_ref[row : row + 1, :], 0.0)
                block = jnp.where(column < line, block, inner)
        denominator = (
            column_ref[left, rows, :]
            + level_ref[right : right + 1, :]
            - occupied[left]
            - occupied[right]
        )
        ratio = block / denominator
        ratio_ref[index] = ratio
        times = jnp.where(column == line, 1.0, 2.0) if left == right else 1.0
        energy_table[index] = jnp.sum(times * block * ratio)
        weight = weight_table[left * list_width + right]
        if left != right:
            weight = weight + weight_table[right * list_width + left]
        squares = times * (weight.astype(F32) / width) * (ratio * ratio)
        row_squares[left] = row_squares[left] + squares
        acc_ref[right : right + 1, :] += jnp.sum(squares, axis=0, keepdims=True)
    for s in range(list_width):
        place_ref[rows, :] = row_squares[s]
        acc_ref[s : s + 1, :] += jnp.sum(place_ref[...].T, axis=0, keepdims=True)

    def block_of(pair):
        low = jnp.minimum(packed[pair, 0], packed[pair, 1])
        high = jnp.maximum(packed[pair, 0], packed[pair, 1])
        return jnp.where(low == 0, 0, jnp.where(low == 1, 3, jnp.where(low == 2, 5, 6))) + high

    lane = lax.broadcasted_iota(jnp.int32, (1, width), 1)
    energies = jnp.zeros((1, width), F32)
    for pair in range(pairs):
        energy = -packed[pair, 2].astype(F32) * energy_table[block_of(pair)] / (width * width)
        energies = jnp.where(lane == pair, energy, energies)
    share = pairs // list_width
    for quarter in range(list_width):
        lines = split(acc_ref[quarter : quarter + 1, :]) + split(energies)
        lines.append(jnp.zeros((TAIL - len(lines), width), F32))
        tail = jnp.concatenate(lines, axis=0).astype(jnp.bfloat16)
        out_ref[quarter, share * depth :, :] = tail
    for pair in range(pairs):
        quarter, k = pair // share, pair % share
        live = (packed[pair, 2] > 0).astype(F32)
        value = (-ratio_ref[block_of(pair)] * live).astype(jnp.bfloat16)
        out_ref[quarter, k * depth : (k + 1) * depth, :] = value


def pair_terms(blocks, levels, packed, occupied, place):
    height, width = blocks.shape
    depth = (height - 8) // SENT
    list_width = levels.shape[0]
    whole = pl.BlockSpec(memory_space=pltpu.VMEM)
    scalar = pl.BlockSpec(memory_space=pltpu.SMEM)
    rows = packed.shape[0] // list_width * depth + TAIL
    return pl.pallas_call(
        pair_kernel,
        out_shape=jax.ShapeDtypeStruct((list_width, rows, width), jnp.bfloat16),
        in_specs=[scalar, scalar, scalar, whole, whole],
        out_specs=whole,
        scratch_shapes=[
            pltpu.VMEM((len(BLOCKS), depth, width), F32),
            pltpu.VMEM((list_width, width, width), F32),
            pltpu.VMEM((width, width), F32),
            pltpu.VMEM((list_width, width), F32),
            pltpu.SMEM((list_width * list_width,), jnp.int32),
            pltpu.SMEM((len(BLOCKS),), F32),
        ],
        compiler_params=pltpu.CompilerParams(vmem_limit_bytes=VMEM_LIMIT),
        name="pair_terms",
    )(packed, occupied, place, blocks, levels)


def plane_kernel(parts_ref, out_ref):
    owners, height, width = parts_ref.shape
    body = height - TAIL
    tails = [parts_ref[s, body:, :].astype(F32) for s in range(owners)]
    vectors = [tails[s][k : k + 1] for k in range(3) for s in range(owners)]
    per_zone = out_ref.shape[0] // owners
    for s in range(owners):
        lines = vectors + [tails[s][3:6], jnp.zeros((TAIL - 3 * owners - 3, width), F32)]
        tail = jnp.concatenate(lines, axis=0).astype(jnp.bfloat16)
        for k in range(per_zone):
            out_ref[s * per_zone + k, :body, :] = parts_ref[s, :body, :]
            out_ref[s * per_zone + k, body:, :] = tail


def plane_terms(parts, planes):
    whole = pl.BlockSpec(memory_space=pltpu.VMEM)
    return pl.pallas_call(
        plane_kernel,
        out_shape=jax.ShapeDtypeStruct((planes,) + parts.shape[1:], parts.dtype),
        in_specs=[whole],
        out_specs=whole,
        compiler_params=pltpu.CompilerParams(vmem_limit_bytes=VMEM_LIMIT),
        name="plane_terms",
    )(parts)


def owner_kernel(place, parts_ref, terms_ref, energy_ref):
    planes, height, width = parts_ref.shape
    share = energy_ref.shape[0]
    body = height - TAIL
    sums = []
    for low in range(2):
        total = None
        for q in range(planes // 2):
            tail = parts_ref[q * 2 + low, body:, :].astype(F32)
            vectors = tail[0:4] + (tail[4:8] + tail[8:12])
            total = vectors if total is None else total + vectors
        sums.append(total)
    tile = jnp.concatenate(sums, axis=0)
    for k in range(terms_ref.shape[0] // 8):
        terms_ref[8 * k : 8 * k + 8, :] = tile
    energies = jnp.zeros((1, width), F32)
    for q in range(planes // 2):
        tail = parts_ref[q * 2 + place[1], body:, :].astype(F32)
        energies = energies + (tail[12:13] + (tail[13:14] + tail[14:15]))
    lane = lax.broadcasted_iota(jnp.int32, (1, width), 1)
    for k in range(share):
        energy_ref[k] = jnp.sum(jnp.where(lane == place[2] * share + k, energies, 0.0))


def owner_terms(parts, place, lines, share):
    whole = pl.BlockSpec(memory_space=pltpu.VMEM)
    scalar = pl.BlockSpec(memory_space=pltpu.SMEM)
    return pl.pallas_call(
        owner_kernel,
        out_shape=(
            jax.ShapeDtypeStruct((lines, parts.shape[2]), F32),
            jax.ShapeDtypeStruct((share,), F32),
        ),
        in_specs=[scalar, whole],
        out_specs=(whole, scalar),
        compiler_params=pltpu.CompilerParams(vmem_limit_bytes=VMEM_LIMIT),
        name="owner_terms",
    )(place, parts)


def join_kernel(slots, place, parts_ref, out_ref):
    share, width, _ = out_ref.shape
    sources, height, _ = parts_ref.shape
    depth = (height - TAIL) // share
    line = lax.broadcasted_iota(jnp.int32, (width, width), 0)
    column = lax.broadcasted_iota(jnp.int32, (width, width), 1)
    for k in range(share):
        block = jnp.concatenate(
            [
                parts_ref[q * 2 + place[1], k * depth : (k + 1) * depth, :].astype(F32)
                for q in range(sources // 2)
            ],
            axis=0,
        )
        pair = place[2] * share + k
        swapped = slots[pair, 0] > slots[pair, 1]
        same = slots[pair, 0] == slots[pair, 1]
        other = block.T
        both = jnp.where(line == column, block, block + other)
        value = jnp.where(same, both, jnp.where(swapped, other, block))
        out_ref[k] = value.astype(jnp.bfloat16)


def join_amplitudes(parts, pair_slots, place, share):
    whole = pl.BlockSpec(memory_space=pltpu.VMEM)
    scalar = pl.BlockSpec(memory_space=pltpu.SMEM)
    width = parts.shape[2]
    return pl.pallas_call(
        join_kernel,
        out_shape=jax.ShapeDtypeStruct((share, width, width), jnp.bfloat16),
        in_specs=[scalar, scalar, whole],
        out_specs=whole,
        compiler_params=pltpu.CompilerParams(vmem_limit_bytes=VMEM_LIMIT),
        name="join_amplitudes",
    )(pair_slots, place, parts)


def grad_kernel(owner_ref, terms_ref, out_ref):
    occ_local = out_ref.shape[0]
    lines = owner_ref.shape[1]
    chosen = (
        lax.broadcasted_iota(jnp.int32, (occ_local, lines), 0) == owner_ref[...]
    ).astype(F32)
    out_ref[...] = jnp.dot(
        chosen, terms_ref[...], preferred_element_type=F32, precision=lax.Precision.HIGHEST
    )


def sum_grads(terms, line_owner, occ_local):
    whole = pl.BlockSpec(memory_space=pltpu.VMEM)
    return pl.pallas_call(
        grad_kernel,
        out_shape=jax.ShapeDtypeStruct((occ_local, terms.shape[1]), F32),
        in_specs=[whole, whole],
        out_specs=whole,
        compiler_params=pltpu.CompilerParams(vmem_limit_bytes=VMEM_LIMIT),
        name="sum_grads",
    )(line_owner, terms)


def on_device(
    half_integrals,
    domain_map,
    domain_index,
    owner_orbitals,
    pair_slots,
    pair_weight,
    virtual_energy,
    occupied_energy,
):
    position = {name: lax.axis_index(name) for name in AXES}
    size = {name: lax.axis_size(name) for name in AXES}
    x = position["x"]

    def aux_rank(zh):
        rank = zh
        for name in AXES[1:-1]:
            rank = rank * size[name] + position[name]
        return rank

    occ_local, rows, width = half_integrals.shape
    owners, list_width = owner_orbitals.shape
    share = pair_slots.shape[0] // size["x"]
    cross = [(q * 4 + s, s * 4 + q) for q in range(4) for s in range(4)]

    packed = lax.ppermute(
        jnp.concatenate([pair_slots, pair_weight[:, None]], axis=1), ("zh", "x"), cross
    )
    own = lax.dynamic_slice_in_dim(owner_orbitals, x, 1, 1)[:, 0] - x * occ_local
    grid = own.reshape([size[name] for name in AXES[:-1]])
    line_owner = grid.transpose(2, 3, 4, 1, 0).reshape(1, -1)

    my_orbitals = lax.dynamic_slice_in_dim(owner_orbitals, aux_rank(x), 1, 0)[0]
    my_index = domain_index[my_orbitals]
    virt_count = virtual_energy.shape[0]
    levels = jnp.where(
        my_index >= 0, virtual_energy[jnp.clip(my_index, 0, virt_count - 1)], jnp.float32(1.0)
    )
    occupied = occupied_energy[my_orbitals]

    outgoing = make_slabs(half_integrals, domain_map, domain_index, owner_orbitals, x)
    inner = ("zl", "yl", "c", "x")
    members = size["zl"] * size["yl"] * size["c"] * size["x"]
    per_member = owners // members
    received = lax.all_to_all(
        outgoing.reshape(members, per_member * width, rows),
        inner,
        split_axis=0,
        concat_axis=0,
        tiled=True,
    )
    scaled = partial_grams(
        received.reshape(members // size["x"], list_width, per_member, width, rows)
    )
    depth = scaled.shape[2]
    sent = scaled.astype(jnp.float16).reshape(-1, depth, width)
    arrived = lax.all_to_all(sent, ("zh", "yh"), split_axis=0, concat_axis=0, tiled=True)
    power = arrived[:, depth - 1 :, :].astype(F32) - TOP_POWER
    blocks = jnp.sum(arrived[:, : depth - 8, :].astype(F32) * jnp.exp2(power), axis=0)

    place = jnp.stack([position["zh"], position["zl"], x]).astype(jnp.int32)
    slices = pair_terms(blocks, levels, packed, occupied, place)
    slices = lax.all_to_all(slices, "x", split_axis=0, concat_axis=0, tiled=True)
    planes = plane_terms(slices, size["zh"] * size["zl"])
    parts = lax.all_to_all(planes, ("zh", "zl"), split_axis=0, concat_axis=0, tiled=True)
    lines, pair_energy = owner_terms(parts, place, owners, share)
    all_lines = lax.all_to_all(lines, ("yh", "yl", "c"), split_axis=0, concat_axis=0, tiled=True)
    amplitude = join_amplitudes(parts, pair_slots, place, share)
    domain_grad = sum_grads(all_lines, line_owner, occ_local)
    return (amplitude, pair_energy, domain_grad)


def solution(mesh):
    fine = jax.sharding.Mesh(mesh.devices.reshape(4, 2, 4, 2, 2, 4), AXES)
    aux, orb = AXES[:-1], "x"
    placed = (
        P(orb, aux, None),
        P(orb, None, None),
        P(),
        P(),
        P(aux, None),
        P(aux),
        P(),
        P(),
    )
    return jax.shard_map(
        on_device,
        mesh=fine,
        in_specs=placed,
        out_specs=(P(AXES, None, None), P(AXES), P(orb, None)),
        check_vma=False,
    )
```

```python
import functools

import jax
import jax.numpy as jnp
from jax import lax
from jax.experimental import pallas as pl
from jax.experimental.pallas import tpu as pltpu
from jax.sharding import PartitionSpec as P

F32 = jnp.float32
VMEM_LIMIT = 48 * 1024 * 1024
SLAB_VMEM_LIMIT = 62 * 1024 * 1024
OWNERS_PER_STEP = 32
ORBS_PER_STEP = 16
GRAMS_PER_STEP = 2
AXES = ("zh", "zl", "yh", "yl", "c", "x")
BLOCKS = tuple((s, t) for s in range(4) for t in range(s, 4))
CROSS = tuple((s, t) for s, t in BLOCKS if s < t)
SENT = len(CROSS) + 2
TAIL = 16
TOP_POWER = 14.0


def slab_kernel(owner_list, group, integral_ref, map_ref, index_ref, out_ref, slab_ref):
    orbs = integral_ref.shape[0]
    occ_local = slab_ref.shape[0]
    per_step = out_ref.shape[0]
    step = pl.program_id(0)
    first_write = occ_local // orbs
    first_orb = group[0] * occ_local

    @pl.when(step < first_write)
    def _():
        for k in range(orbs):
            orb = step * orbs + k
            live = index_ref[pl.ds(first_orb + orb, 1), :] >= 0
            masked = map_ref[k] * live.astype(F32).astype(jnp.bfloat16)
            slab_ref[orb] = lax.dot_general(
                masked.T, integral_ref[k], (((1,), (1,)), ((), ())), preferred_element_type=F32
            ).astype(jnp.bfloat16)

    @pl.when(step >= first_write)
    def _():
        part = step - first_write
        base = jnp.right_shift(part, 1) * 16 + jnp.bitwise_and(part, 1) * 2
        for k in range(per_step):
            owner = base + (k % 4) * 32 + (k // 4 % 4) * 4 + k // 16
            out_ref[k] = slab_ref[owner_list[group[0], owner] - first_orb]


def make_slabs(half_integrals, domain_map, domain_index, owner_orbitals, orb_group):
    occ_local, rows, width = half_integrals.shape
    owners = owner_orbitals.shape[0]
    parts = occ_local // ORBS_PER_STEP
    read = lambda i, s, t: (jnp.minimum(i, parts - 1), 0, 0)
    return pl.pallas_call(
        slab_kernel,
        out_shape=jax.ShapeDtypeStruct((owners, width, rows), jnp.bfloat16),
        grid_spec=pltpu.PrefetchScalarGridSpec(
            num_scalar_prefetch=2,
            grid=(parts + owners // OWNERS_PER_STEP,),
            in_specs=[
                pl.BlockSpec((ORBS_PER_STEP, rows, width), read),
                pl.BlockSpec((ORBS_PER_STEP, width, width), read),
                pl.BlockSpec(domain_index.shape, lambda i, s, t: (0, 0)),
            ],
            out_specs=pl.BlockSpec(
                (OWNERS_PER_STEP, width, rows), lambda i, s, t: (jnp.maximum(i - parts, 0), 0, 0)
            ),
            scratch_shapes=[pltpu.VMEM((occ_local, width, rows), jnp.bfloat16)],
        ),
        compiler_params=pltpu.CompilerParams(vmem_limit_bytes=SLAB_VMEM_LIMIT),
        name="slabs",
    )(
        owner_orbitals.T,
        orb_group[None].astype(jnp.int32),
        half_integrals,
        domain_map,
        domain_index,
    )


def gram_kernel(slab_ref, out_ref):
    count, list_width, owners, width, rows = slab_ref.shape
    half = list_width * width // 2
    middle = list_width // 2
    product = functools.partial(
        lax.dot_general,
        dimension_numbers=(((1,), (1,)), ((), ())),
        preferred_element_type=F32,
    )
    pieces = out_ref.shape[1]
    depth = width // pieces
    base = SENT * depth
    line = lax.broadcasted_iota(jnp.int32, (width, width), 0)
    lane = lax.broadcasted_iota(jnp.int32, (width, width), 1)
    for j in range(owners):
        low = jnp.concatenate(
            [slab_ref[k, :middle, j].reshape(half, rows) for k in range(count)], axis=1
        )
        high = jnp.concatenate(
            [slab_ref[k, middle:, j].reshape(half, rows) for k in range(count)], axis=1
        )
        parts = (product(low, low), product(low, high), product(high, high))

        def block_at(left, right):
            row, column = left % 2 * width, right % 2 * width
            return parts[left // 2 + right // 2][row : row + width, column : column + width]

        top = jnp.zeros((8, width), F32)
        for s in range(list_width):
            top = jnp.maximum(
                top, jnp.max(jnp.abs(block_at(s, s)).reshape(width // 8, 8, width), axis=0)
            )
        top = jnp.max(jnp.max(top, axis=0, keepdims=True), axis=1, keepdims=True)
        power = jnp.clip(jnp.ceil(jnp.log2(jnp.maximum(top, 1e-35))), -100.0, 100.0)
        power = jnp.broadcast_to(power, (8, width))
        scale = jnp.exp2(TOP_POWER - power)[0:1]
        blocks = [block_at(left, right) for left, right in CROSS]
        diagonals = []
        for s in range(0, list_width, 2):
            lower = block_at(s + 1, s + 1)
            blocks.append(jnp.where(lane >= line, block_at(s, s), lower))
            diagonals.append(
                jnp.sum(jnp.where(lane == line, lower, 0.0), axis=0, keepdims=True) * scale
            )
        tail = jnp.concatenate(diagonals + [power[: 8 - len(diagonals)]], axis=0)
        for index, block in enumerate(blocks):
            block = block * scale
            for q in range(pieces):
                out_ref[j, q, index * depth : (index + 1) * depth, :] = block[
                    q * depth : (q + 1) * depth
                ]
        for q in range(pieces):
            out_ref[j, q, base : base + 8, :] = tail
            out_ref[j, q, base + 8 : base + TAIL, :] = power


def partial_grams(slabs):
    count, list_width, owners, width, rows = slabs.shape
    pieces = 4
    depth = SENT * (width // pieces) + TAIL
    return pl.pallas_call(
        gram_kernel,
        out_shape=jax.ShapeDtypeStruct((owners, pieces, depth, width), F32),
        grid=(owners // GRAMS_PER_STEP,),
        in_specs=[
            pl.BlockSpec(
                (count, list_width, GRAMS_PER_STEP, width, rows), lambda j: (0, 0, j, 0, 0)
            )
        ],
        out_specs=pl.BlockSpec((GRAMS_PER_STEP, pieces, depth, width), lambda j: (j, 0, 0, 0)),
        compiler_params=pltpu.CompilerParams(vmem_limit_bytes=VMEM_LIMIT),
        name="partial_grams",
    )(slabs)


def split(value):
    high = value.astype(jnp.bfloat16).astype(F32)
    middle = (value - high).astype(jnp.bfloat16).astype(F32)
    return [high, middle, value - high - middle]


def pair_kernel(
    packed,
    occupied,
    place,
    block_ref,
    level_ref,
    out_ref,
    ratio_ref,
    column_ref,
    place_ref,
    acc_ref,
    weight_table,
    energy_table,
):
    list_width, width = level_ref.shape
    depth = (block_ref.shape[0] - 8) // SENT
    pairs = packed.shape[0]
    piece = place[0]
    rows = pl.ds(pl.multiple_of(piece * depth, depth), depth)
    for k in range(list_width * list_width):
        weight_table[k] = 0
    for pair in range(pairs):
        weight_table[packed[pair, 0] * list_width + packed[pair, 1]] = packed[pair, 2]
    for s in range(list_width):
        column_ref[s] = jnp.broadcast_to(level_ref[s : s + 1, :], (width, width)).T
    acc_ref[...] = jnp.zeros_like(acc_ref)
    place_ref[...] = jnp.zeros_like(place_ref)
    row_squares = [jnp.zeros((depth, width), F32) for _ in range(list_width)]
    line = lax.broadcasted_iota(jnp.int32, (depth, width), 0) + piece * depth
    column = lax.broadcasted_iota(jnp.int32, (depth, width), 1)

    def block_at(index):
        return block_ref[index * depth : (index + 1) * depth, :]

    for index, (left, right) in enumerate(BLOCKS):
        if left != right:
            block = block_at(CROSS.index((left, right)))
        else:
            block = block_at(len(CROSS) + left // 2)
            if left % 2 == 0:
                block = jnp.where(column >= line, block, 0.0)
            else:
                row = SENT * depth + left // 2
                inner = jnp.where(column == line, block_ref[row : row + 1, :], 0.0)
                block = jnp.where(column < line, block, inner)
        denominator = (
            column_ref[left, rows, :]
            + level_ref[right : right + 1, :]
            - occupied[left]
            - occupied[right]
        )
        ratio = block / denominator
        ratio_ref[index] = ratio
        times = jnp.where(column == line, 1.0, 2.0) if left == right else 1.0
        energy_table[index] = jnp.sum(times * block * ratio)
        weight = weight_table[left * list_width + right]
        if left != right:
            weight = weight + weight_table[right * list_width + left]
        squares = times * (weight.astype(F32) / width) * (ratio * ratio)
        row_squares[left] = row_squares[left] + squares
        acc_ref[right : right + 1, :] += jnp.sum(squares, axis=0, keepdims=True)
    for s in range(list_width):
        place_ref[rows, :] = row_squares[s]
        acc_ref[s : s + 1, :] += jnp.sum(place_ref[...].T, axis=0, keepdims=True)

    def block_of(pair):
        low = jnp.minimum(packed[pair, 0], packed[pair, 1])
        high = jnp.maximum(packed[pair, 0], packed[pair, 1])
        return jnp.where(low == 0, 0, jnp.where(low == 1, 3, jnp.where(low == 2, 5, 6))) + high

    lane = lax.broadcasted_iota(jnp.int32, (1, width), 1)
    energies = jnp.zeros((1, width), F32)
    for pair in range(pairs):
        energy = -packed[pair, 2].astype(F32) * energy_table[block_of(pair)] / (width * width)
        energies = jnp.where(lane == pair, energy, energies)
    share = pairs // list_width
    for quarter in range(list_width):
        lines = split(acc_ref[quarter : quarter + 1, :]) + split(energies)
        lines.append(jnp.zeros((TAIL - len(lines), width), F32))
        tail = jnp.concatenate(lines, axis=0).astype(jnp.bfloat16)
        out_ref[quarter, share * depth :, :] = tail
    for pair in range(pairs):
        quarter, k = pair // share, pair % share
        live = (packed[pair, 2] > 0).astype(F32)
        value = (-ratio_ref[block_of(pair)] * live).astype(jnp.bfloat16)
        out_ref[quarter, k * depth : (k + 1) * depth, :] = value


def pair_terms(blocks, levels, packed, occupied, place):
    height, width = blocks.shape
    depth = (height - 8) // SENT
    list_width = levels.shape[0]
    whole = pl.BlockSpec(memory_space=pltpu.VMEM)
    scalar = pl.BlockSpec(memory_space=pltpu.SMEM)
    rows = packed.shape[0] // list_width * depth + TAIL
    return pl.pallas_call(
        pair_kernel,
        out_shape=jax.ShapeDtypeStruct((list_width, rows, width), jnp.bfloat16),
        in_specs=[scalar, scalar, scalar, whole, whole],
        out_specs=whole,
        scratch_shapes=[
            pltpu.VMEM((len(BLOCKS), depth, width), F32),
            pltpu.VMEM((list_width, width, width), F32),
            pltpu.VMEM((width, width), F32),
            pltpu.VMEM((list_width, width), F32),
            pltpu.SMEM((list_width * list_width,), jnp.int32),
            pltpu.SMEM((len(BLOCKS),), F32),
        ],
        compiler_params=pltpu.CompilerParams(vmem_limit_bytes=VMEM_LIMIT),
        name="pair_terms",
    )(packed, occupied, place, blocks, levels)


def plane_kernel(parts_ref, out_ref):
    owners, height, width = parts_ref.shape
    body = height - TAIL
    tails = [parts_ref[s, body:, :].astype(F32) for s in range(owners)]
    vectors = [tails[s][k : k + 1] for k in range(3) for s in range(owners)]
    per_zone = out_ref.shape[0] // owners
    for s in range(owners):
        lines = vectors + [tails[s][3:6], jnp.zeros((TAIL - 3 * owners - 3, width), F32)]
        tail = jnp.concatenate(lines, axis=0).astype(jnp.bfloat16)
        for k in range(per_zone):
            out_ref[s * per_zone + k, :body, :] = parts_ref[s, :body, :]
            out_ref[s * per_zone + k, body:, :] = tail


def plane_terms(parts, planes):
    whole = pl.BlockSpec(memory_space=pltpu.VMEM)
    return pl.pallas_call(
        plane_kernel,
        out_shape=jax.ShapeDtypeStruct((planes,) + parts.shape[1:], parts.dtype),
        in_specs=[whole],
        out_specs=whole,
        compiler_params=pltpu.CompilerParams(vmem_limit_bytes=VMEM_LIMIT),
        name="plane_terms",
    )(parts)


def owner_kernel(parts_ref, terms_ref):
    planes, height, width = parts_ref.shape
    body = height - TAIL
    sums = []
    for low in range(2):
        total = None
        for q in range(planes // 2):
            tail = parts_ref[q * 2 + low, body:, :].astype(F32)
            vectors = tail[0:4] + (tail[4:8] + tail[8:12])
            total = vectors if total is None else total + vectors
        sums.append(total)
    tile = jnp.concatenate(sums, axis=0)
    for k in range(terms_ref.shape[0] // 8):
        terms_ref[8 * k : 8 * k + 8, :] = tile


def owner_terms(parts, lines):
    whole = pl.BlockSpec(memory_space=pltpu.VMEM)
    return pl.pallas_call(
        owner_kernel,
        out_shape=jax.ShapeDtypeStruct((lines, parts.shape[2]), F32),
        in_specs=[whole],
        out_specs=whole,
        compiler_params=pltpu.CompilerParams(vmem_limit_bytes=VMEM_LIMIT),
        name="owner_terms",
    )(parts)


def join_kernel(slots, place, parts_ref, out_ref, energy_ref):
    share, width, _ = out_ref.shape
    sources, height, _ = parts_ref.shape
    depth = (height - TAIL) // share
    line = lax.broadcasted_iota(jnp.int32, (width, width), 0)
    column = lax.broadcasted_iota(jnp.int32, (width, width), 1)
    energies = jnp.zeros((1, width), F32)
    for q in range(sources // 2):
        tail = parts_ref[q * 2 + place[1], height - TAIL :, :].astype(F32)
        energies = energies + (tail[12:13] + (tail[13:14] + tail[14:15]))
    for k in range(share):
        block = jnp.concatenate(
            [
                parts_ref[q * 2 + place[1], k * depth : (k + 1) * depth, :].astype(F32)
                for q in range(sources // 2)
            ],
            axis=0,
        )
        pair = place[2] * share + k
        swapped = slots[pair, 0] > slots[pair, 1]
        same = slots[pair, 0] == slots[pair, 1]
        other = block.T
        both = jnp.where(line == column, block, block + other)
        value = jnp.where(same, both, jnp.where(swapped, other, block))
        out_ref[k] = value.astype(jnp.bfloat16)
        energy_ref[k] = jnp.sum(jnp.where(column[0:1] == pair, energies, 0.0))


def join_amplitudes(parts, pair_slots, place, share):
    whole = pl.BlockSpec(memory_space=pltpu.VMEM)
    scalar = pl.BlockSpec(memory_space=pltpu.SMEM)
    width = parts.shape[2]
    return pl.pallas_call(
        join_kernel,
        out_shape=(
            jax.ShapeDtypeStruct((share, width, width), jnp.bfloat16),
            jax.ShapeDtypeStruct((share,), F32),
        ),
        in_specs=[scalar, scalar, whole],
        out_specs=(whole, scalar),
        compiler_params=pltpu.CompilerParams(vmem_limit_bytes=VMEM_LIMIT),
        name="join_amplitudes",
    )(pair_slots, place, parts)


def grad_kernel(owner_ref, terms_ref, out_ref):
    occ_local = out_ref.shape[0]
    lines = owner_ref.shape[1]
    chosen = (
        lax.broadcasted_iota(jnp.int32, (occ_local, lines), 0) == owner_ref[...]
    ).astype(F32)
    out_ref[...] = jnp.dot(
        chosen, terms_ref[...], preferred_element_type=F32, precision=lax.Precision.HIGHEST
    )


def sum_grads(terms, line_owner, occ_local):
    whole = pl.BlockSpec(memory_space=pltpu.VMEM)
    return pl.pallas_call(
        grad_kernel,
        out_shape=jax.ShapeDtypeStruct((occ_local, terms.shape[1]), F32),
        in_specs=[whole, whole],
        out_specs=whole,
        compiler_params=pltpu.CompilerParams(vmem_limit_bytes=VMEM_LIMIT),
        name="sum_grads",
    )(line_owner, terms)


def on_device(
    half_integrals,
    domain_map,
    domain_index,
    owner_orbitals,
    pair_slots,
    pair_weight,
    virtual_energy,
    occupied_energy,
):
    position = {name: lax.axis_index(name) for name in AXES}
    size = {name: lax.axis_size(name) for name in AXES}
    x = position["x"]

    def aux_rank(yh):
        rank = 0
        for name in AXES[:-1]:
            rank = rank * size[name] + (yh if name == "yh" else position[name])
        return rank

    occ_local, rows, width = half_integrals.shape
    owners, list_width = owner_orbitals.shape
    share = pair_slots.shape[0] // size["x"]
    cross = [(q * 4 + s, s * 4 + q) for q in range(4) for s in range(4)]

    packed = lax.ppermute(
        jnp.concatenate([pair_slots, pair_weight[:, None]], axis=1), ("yh", "x"), cross
    )
    own = lax.dynamic_slice_in_dim(owner_orbitals, x, 1, 1)[:, 0] - x * occ_local
    grid = own.reshape([size[name] for name in AXES[:-1]])
    line_owner = grid.transpose(0, 1, 4, 3, 2).reshape(1, -1)

    my_orbitals = lax.dynamic_slice_in_dim(owner_orbitals, aux_rank(x), 1, 0)[0]
    my_index = domain_index[my_orbitals]
    virt_count = virtual_energy.shape[0]
    levels = jnp.where(
        my_index >= 0, virtual_energy[jnp.clip(my_index, 0, virt_count - 1)], jnp.float32(1.0)
    )
    occupied = occupied_energy[my_orbitals]

    outgoing = make_slabs(half_integrals, domain_map, domain_index, owner_orbitals, x)
    inner = ("zl", "yl", "c", "x")
    members = size["zl"] * size["yl"] * size["c"] * size["x"]
    per_member = owners // members
    received = lax.all_to_all(
        outgoing.reshape(members, per_member * width, rows),
        inner,
        split_axis=0,
        concat_axis=0,
        tiled=True,
    )
    scaled = partial_grams(
        received.reshape(members // size["x"], list_width, per_member, width, rows)
    )
    depth = scaled.shape[2]
    sent = scaled.astype(jnp.float16).reshape(-1, depth, width)
    arrived = lax.all_to_all(sent, ("zh", "yh"), split_axis=0, concat_axis=0, tiled=True)
    power = arrived[:, depth - 1 :, :].astype(F32) - TOP_POWER
    blocks = jnp.sum(arrived[:, : depth - 8, :].astype(F32) * jnp.exp2(power), axis=0)

    place = jnp.stack([position["yh"], position["yl"], x]).astype(jnp.int32)
    slices = pair_terms(blocks, levels, packed, occupied, place)
    slices = lax.all_to_all(slices, "x", split_axis=0, concat_axis=0, tiled=True)
    planes = plane_terms(slices, size["yh"] * size["yl"])
    parts = lax.all_to_all(planes, ("yh", "yl"), split_axis=0, concat_axis=0, tiled=True)
    lines = owner_terms(parts, owners)
    all_lines = lax.all_to_all(lines, ("zh", "zl", "c"), split_axis=0, concat_axis=0, tiled=True)
    amplitude, pair_energy = join_amplitudes(parts, pair_slots, place, share)
    domain_grad = sum_grads(all_lines, line_owner, occ_local)
    return (amplitude, pair_energy, domain_grad)


def solution(mesh):
    fine = jax.sharding.Mesh(mesh.devices.reshape(4, 2, 4, 2, 2, 4), AXES)
    aux, orb = AXES[:-1], "x"
    placed = (
        P(orb, aux, None),
        P(orb, None, None),
        P(),
        P(),
        P(aux, None),
        P(aux),
        P(),
        P(),
    )
    return jax.shard_map(
        on_device,
        mesh=fine,
        in_specs=placed,
        out_specs=(P(AXES, None, None), P(AXES), P(orb, None)),
        check_vma=False,
    )
```

```python
import functools

import jax
import jax.numpy as jnp
from jax import lax
from jax.experimental import pallas as pl
from jax.experimental.pallas import tpu as pltpu
from jax.sharding import PartitionSpec as P

F32 = jnp.float32
VMEM_LIMIT = 48 * 1024 * 1024
SLAB_VMEM_LIMIT = 62 * 1024 * 1024
OWNERS_PER_STEP = 32
ORBS_PER_STEP = 16
GRAMS_PER_STEP = 2
AXES = ("zh", "zl", "yh", "yl", "c", "x")
BLOCKS = tuple((s, t) for s in range(4) for t in range(s, 4))
CROSS = tuple((s, t) for s, t in BLOCKS if s < t)
SENT = len(CROSS) + 2
TAIL = 16
TOP_POWER = 14.0


def slab_kernel(owner_list, group, integral_ref, map_ref, index_ref, out_ref, slab_ref):
    orbs = integral_ref.shape[0]
    occ_local = slab_ref.shape[0]
    per_step = out_ref.shape[0]
    step = pl.program_id(0)
    first_write = occ_local // orbs
    first_orb = group[0] * occ_local

    @pl.when(step < first_write)
    def _():
        for k in range(orbs):
            orb = step * orbs + k
            live = index_ref[pl.ds(first_orb + orb, 1), :] >= 0
            masked = map_ref[k] * live.astype(F32).astype(jnp.bfloat16)
            slab_ref[orb] = lax.dot_general(
                masked.T, integral_ref[k], (((1,), (1,)), ((), ())), preferred_element_type=F32
            ).astype(jnp.bfloat16)

    @pl.when(step >= first_write)
    def _():
        part = step - first_write
        base = jnp.right_shift(part, 1) * 16 + jnp.bitwise_and(part, 1) * 2
        for k in range(per_step):
            owner = base + (k % 4) * 32 + (k // 4 % 4) * 4 + k // 16
            out_ref[k] = slab_ref[owner_list[group[0], owner] - first_orb]


def make_slabs(half_integrals, domain_map, domain_index, owner_orbitals, orb_group):
    occ_local, rows, width = half_integrals.shape
    owners = owner_orbitals.shape[0]
    parts = occ_local // ORBS_PER_STEP
    read = lambda i, s, t: (jnp.minimum(i, parts - 1), 0, 0)
    return pl.pallas_call(
        slab_kernel,
        out_shape=jax.ShapeDtypeStruct((owners, width, rows), jnp.bfloat16),
        grid_spec=pltpu.PrefetchScalarGridSpec(
            num_scalar_prefetch=2,
            grid=(parts + owners // OWNERS_PER_STEP,),
            in_specs=[
                pl.BlockSpec((ORBS_PER_STEP, rows, width), read),
                pl.BlockSpec((ORBS_PER_STEP, width, width), read),
                pl.BlockSpec(domain_index.shape, lambda i, s, t: (0, 0)),
            ],
            out_specs=pl.BlockSpec(
                (OWNERS_PER_STEP, width, rows), lambda i, s, t: (jnp.maximum(i - parts, 0), 0, 0)
            ),
            scratch_shapes=[pltpu.VMEM((occ_local, width, rows), jnp.bfloat16)],
        ),
        compiler_params=pltpu.CompilerParams(vmem_limit_bytes=SLAB_VMEM_LIMIT),
        name="slabs",
    )(
        owner_orbitals.T,
        orb_group[None].astype(jnp.int32),
        half_integrals,
        domain_map,
        domain_index,
    )


def gram_kernel(slab_ref, out_ref):
    count, list_width, owners, width, rows = slab_ref.shape
    half = list_width * width // 2
    middle = list_width // 2
    product = functools.partial(
        lax.dot_general,
        dimension_numbers=(((1,), (1,)), ((), ())),
        preferred_element_type=F32,
    )
    pieces = out_ref.shape[1]
    depth = width // pieces
    base = SENT * depth
    line = lax.broadcasted_iota(jnp.int32, (width, width), 0)
    lane = lax.broadcasted_iota(jnp.int32, (width, width), 1)
    for j in range(owners):
        low = jnp.concatenate(
            [slab_ref[k, :middle, j].reshape(half, rows) for k in range(count)], axis=1
        )
        high = jnp.concatenate(
            [slab_ref[k, middle:, j].reshape(half, rows) for k in range(count)], axis=1
        )
        parts = (product(low, low), product(low, high), product(high, high))

        def block_at(left, right):
            row, column = left % 2 * width, right % 2 * width
            return parts[left // 2 + right // 2][row : row + width, column : column + width]

        top = jnp.zeros((8, width), F32)
        for s in range(list_width):
            top = jnp.maximum(
                top, jnp.max(jnp.abs(block_at(s, s)).reshape(width // 8, 8, width), axis=0)
            )
        top = jnp.max(jnp.max(top, axis=0, keepdims=True), axis=1, keepdims=True)
        power = jnp.clip(jnp.ceil(jnp.log2(jnp.maximum(top, 1e-35))), -100.0, 100.0)
        power = jnp.broadcast_to(power, (8, width))
        scale = jnp.exp2(TOP_POWER - power)[0:1]
        blocks = [block_at(left, right) for left, right in CROSS]
        diagonals = []
        for s in range(0, list_width, 2):
            lower = block_at(s + 1, s + 1)
            blocks.append(jnp.where(lane >= line, block_at(s, s), lower))
            diagonals.append(
                jnp.sum(jnp.where(lane == line, lower, 0.0), axis=0, keepdims=True) * scale
            )
        tail = jnp.concatenate(diagonals + [power[: 8 - len(diagonals)]], axis=0)
        for index, block in enumerate(blocks):
            block = block * scale
            for q in range(pieces):
                out_ref[j, q, index * depth : (index + 1) * depth, :] = block[
                    q * depth : (q + 1) * depth
                ]
        for q in range(pieces):
            out_ref[j, q, base : base + 8, :] = tail
            out_ref[j, q, base + 8 : base + TAIL, :] = power


def partial_grams(slabs):
    count, list_width, owners, width, rows = slabs.shape
    pieces = 4
    depth = SENT * (width // pieces) + TAIL
    return pl.pallas_call(
        gram_kernel,
        out_shape=jax.ShapeDtypeStruct((owners, pieces, depth, width), F32),
        grid=(owners // GRAMS_PER_STEP,),
        in_specs=[
            pl.BlockSpec(
                (count, list_width, GRAMS_PER_STEP, width, rows), lambda j: (0, 0, j, 0, 0)
            )
        ],
        out_specs=pl.BlockSpec((GRAMS_PER_STEP, pieces, depth, width), lambda j: (j, 0, 0, 0)),
        compiler_params=pltpu.CompilerParams(vmem_limit_bytes=VMEM_LIMIT),
        name="partial_grams",
    )(slabs)


def split(value):
    high = value.astype(jnp.bfloat16).astype(F32)
    middle = (value - high).astype(jnp.bfloat16).astype(F32)
    return [high, middle, value - high - middle]


def pair_kernel(
    packed,
    occupied,
    place,
    block_ref,
    level_ref,
    out_ref,
    ratio_ref,
    column_ref,
    place_ref,
    acc_ref,
    weight_table,
    energy_table,
):
    list_width, width = level_ref.shape
    depth = (block_ref.shape[0] - 8) // SENT
    pairs = packed.shape[0]
    piece = place[0]
    rows = pl.ds(pl.multiple_of(piece * depth, depth), depth)
    for k in range(list_width * list_width):
        weight_table[k] = 0
    for pair in range(pairs):
        weight_table[packed[pair, 0] * list_width + packed[pair, 1]] = packed[pair, 2]
    for s in range(list_width):
        column_ref[s] = jnp.broadcast_to(level_ref[s : s + 1, :], (width, width)).T
    acc_ref[...] = jnp.zeros_like(acc_ref)
    place_ref[...] = jnp.zeros_like(place_ref)
    row_squares = [jnp.zeros((depth, width), F32) for _ in range(list_width)]
    line = lax.broadcasted_iota(jnp.int32, (depth, width), 0) + piece * depth
    column = lax.broadcasted_iota(jnp.int32, (depth, width), 1)

    def block_at(index):
        return block_ref[index * depth : (index + 1) * depth, :]

    for index, (left, right) in enumerate(BLOCKS):
        if left != right:
            block = block_at(CROSS.index((left, right)))
        else:
            block = block_at(len(CROSS) + left // 2)
            if left % 2 == 0:
                block = jnp.where(column >= line, block, 0.0)
            else:
                row = SENT * depth + left // 2
                inner = jnp.where(column == line, block_ref[row : row + 1, :], 0.0)
                block = jnp.where(column < line, block, inner)
        denominator = (
            column_ref[left, rows, :]
            + level_ref[right : right + 1, :]
            - occupied[left]
            - occupied[right]
        )
        ratio = block / denominator
        ratio_ref[index] = ratio
        times = jnp.where(column == line, 1.0, 2.0) if left == right else 1.0
        energy_table[index] = jnp.sum(times * block * ratio)
        weight = weight_table[left * list_width + right]
        if left != right:
            weight = weight + weight_table[right * list_width + left]
        squares = times * (weight.astype(F32) / width) * (ratio * ratio)
        row_squares[left] = row_squares[left] + squares
        acc_ref[right : right + 1, :] += jnp.sum(squares, axis=0, keepdims=True)
    for s in range(list_width):
        place_ref[rows, :] = row_squares[s]
        acc_ref[s : s + 1, :] += jnp.sum(place_ref[...].T, axis=0, keepdims=True)

    def block_of(pair):
        low = jnp.minimum(packed[pair, 0], packed[pair, 1])
        high = jnp.maximum(packed[pair, 0], packed[pair, 1])
        return jnp.where(low == 0, 0, jnp.where(low == 1, 3, jnp.where(low == 2, 5, 6))) + high

    lane = lax.broadcasted_iota(jnp.int32, (1, width), 1)
    energies = jnp.zeros((1, width), F32)
    for pair in range(pairs):
        energy = -packed[pair, 2].astype(F32) * energy_table[block_of(pair)] / (width * width)
        energies = jnp.where(lane == pair, energy, energies)
    share = pairs // list_width
    for quarter in range(list_width):
        lines = split(acc_ref[quarter : quarter + 1, :]) + split(energies)
        lines.append(jnp.zeros((TAIL - len(lines), width), F32))
        tail = jnp.concatenate(lines, axis=0).astype(jnp.bfloat16)
        out_ref[quarter, share * depth :, :] = tail
    for pair in range(pairs):
        quarter, k = pair // share, pair % share
        live = (packed[pair, 2] > 0).astype(F32)
        value = (-ratio_ref[block_of(pair)] * live).astype(jnp.bfloat16)
        out_ref[quarter, k * depth : (k + 1) * depth, :] = value


def pair_terms(blocks, levels, packed, occupied, place):
    height, width = blocks.shape
    depth = (height - 8) // SENT
    list_width = levels.shape[0]
    whole = pl.BlockSpec(memory_space=pltpu.VMEM)
    scalar = pl.BlockSpec(memory_space=pltpu.SMEM)
    rows = packed.shape[0] // list_width * depth + TAIL
    return pl.pallas_call(
        pair_kernel,
        out_shape=jax.ShapeDtypeStruct((list_width, rows, width), jnp.bfloat16),
        in_specs=[scalar, scalar, scalar, whole, whole],
        out_specs=whole,
        scratch_shapes=[
            pltpu.VMEM((len(BLOCKS), depth, width), F32),
            pltpu.VMEM((list_width, width, width), F32),
            pltpu.VMEM((width, width), F32),
            pltpu.VMEM((list_width, width), F32),
            pltpu.SMEM((list_width * list_width,), jnp.int32),
            pltpu.SMEM((len(BLOCKS),), F32),
        ],
        compiler_params=pltpu.CompilerParams(vmem_limit_bytes=VMEM_LIMIT),
        name="pair_terms",
    )(packed, occupied, place, blocks, levels)


def plane_kernel(parts_ref, out_ref):
    owners, height, width = parts_ref.shape
    body = height - TAIL
    tails = [parts_ref[s, body:, :].astype(F32) for s in range(owners)]
    vectors = [tails[s][k : k + 1] for k in range(3) for s in range(owners)]
    for s in range(owners):
        lines = vectors + [tails[s][3:6], jnp.zeros((TAIL - 3 * owners - 3, width), F32)]
        tail = jnp.concatenate(lines, axis=0).astype(jnp.bfloat16)
        out_ref[s, :body, :] = parts_ref[s, :body, :]
        out_ref[s, body:, :] = tail


def plane_terms(parts):
    whole = pl.BlockSpec(memory_space=pltpu.VMEM)
    return pl.pallas_call(
        plane_kernel,
        out_shape=jax.ShapeDtypeStruct(parts.shape, parts.dtype),
        in_specs=[whole],
        out_specs=whole,
        compiler_params=pltpu.CompilerParams(vmem_limit_bytes=VMEM_LIMIT),
        name="plane_terms",
    )(parts)


def owner_kernel(parts_ref, terms_ref):
    pieces, height, width = parts_ref.shape
    total = None
    for q in range(pieces):
        tail = parts_ref[q, height - TAIL :, :].astype(F32)
        vectors = tail[0:4] + (tail[4:8] + tail[8:12])
        total = vectors if total is None else total + vectors
    tile = jnp.concatenate([total, total], axis=0)
    for k in range(terms_ref.shape[0] // 8):
        terms_ref[8 * k : 8 * k + 8, :] = tile


def owner_terms(parts, lines):
    whole = pl.BlockSpec(memory_space=pltpu.VMEM)
    return pl.pallas_call(
        owner_kernel,
        out_shape=jax.ShapeDtypeStruct((lines, parts.shape[2]), F32),
        in_specs=[whole],
        out_specs=whole,
        compiler_params=pltpu.CompilerParams(vmem_limit_bytes=VMEM_LIMIT),
        name="owner_terms",
    )(parts)


def join_kernel(slots, place, parts_ref, out_ref, energy_ref):
    share, width, _ = out_ref.shape
    sources, height, _ = parts_ref.shape
    depth = (height - TAIL) // share
    line = lax.broadcasted_iota(jnp.int32, (width, width), 0)
    column = lax.broadcasted_iota(jnp.int32, (width, width), 1)
    energies = jnp.zeros((1, width), F32)
    for q in range(sources):
        tail = parts_ref[q, height - TAIL :, :].astype(F32)
        energies = energies + (tail[12:13] + (tail[13:14] + tail[14:15]))
    for k in range(share):
        block = jnp.concatenate(
            [
                parts_ref[q, k * depth : (k + 1) * depth, :].astype(F32)
                for q in range(sources)
            ],
            axis=0,
        )
        pair = place[1] * share + k
        swapped = slots[pair, 0] > slots[pair, 1]
        same = slots[pair, 0] == slots[pair, 1]
        other = block.T
        both = jnp.where(line == column, block, block + other)
        value = jnp.where(same, both, jnp.where(swapped, other, block))
        out_ref[k] = value.astype(jnp.bfloat16)
        energy_ref[k] = jnp.sum(jnp.where(column[0:1] == pair, energies, 0.0))


def join_amplitudes(parts, pair_slots, place, share):
    whole = pl.BlockSpec(memory_space=pltpu.VMEM)
    scalar = pl.BlockSpec(memory_space=pltpu.SMEM)
    width = parts.shape[2]
    return pl.pallas_call(
        join_kernel,
        out_shape=(
            jax.ShapeDtypeStruct((share, width, width), jnp.bfloat16),
            jax.ShapeDtypeStruct((share,), F32),
        ),
        in_specs=[scalar, scalar, whole],
        out_specs=(whole, scalar),
        compiler_params=pltpu.CompilerParams(vmem_limit_bytes=VMEM_LIMIT),
        name="join_amplitudes",
    )(pair_slots, place, parts)


def grad_kernel(owner_ref, terms_ref, out_ref):
    occ_local = out_ref.shape[0]
    lines = owner_ref.shape[1]
    chosen = (
        lax.broadcasted_iota(jnp.int32, (occ_local, lines), 0) == owner_ref[...]
    ).astype(F32)
    out_ref[...] = jnp.dot(
        chosen, terms_ref[...], preferred_element_type=F32, precision=lax.Precision.HIGHEST
    )


def sum_grads(terms, line_owner, occ_local):
    whole = pl.BlockSpec(memory_space=pltpu.VMEM)
    return pl.pallas_call(
        grad_kernel,
        out_shape=jax.ShapeDtypeStruct((occ_local, terms.shape[1]), F32),
        in_specs=[whole, whole],
        out_specs=whole,
        compiler_params=pltpu.CompilerParams(vmem_limit_bytes=VMEM_LIMIT),
        name="sum_grads",
    )(line_owner, terms)


def on_device(
    half_integrals,
    domain_map,
    domain_index,
    owner_orbitals,
    pair_slots,
    pair_weight,
    virtual_energy,
    occupied_energy,
):
    position = {name: lax.axis_index(name) for name in AXES}
    size = {name: lax.axis_size(name) for name in AXES}
    x = position["x"]

    def aux_rank(yh):
        rank = 0
        for name in AXES[:-1]:
            rank = rank * size[name] + (yh if name == "yh" else position[name])
        return rank

    occ_local, rows, width = half_integrals.shape
    owners, list_width = owner_orbitals.shape
    share = pair_slots.shape[0] // size["x"]
    cross = [(q * 4 + s, s * 4 + q) for q in range(4) for s in range(4)]

    packed = lax.ppermute(
        jnp.concatenate([pair_slots, pair_weight[:, None]], axis=1), ("yh", "x"), cross
    )
    own = lax.dynamic_slice_in_dim(owner_orbitals, x, 1, 1)[:, 0] - x * occ_local
    grid = own.reshape([size[name] for name in AXES[:-1]])
    line_owner = grid.transpose(0, 1, 3, 4, 2).reshape(1, -1)

    my_orbitals = lax.dynamic_slice_in_dim(owner_orbitals, aux_rank(x), 1, 0)[0]
    my_index = domain_index[my_orbitals]
    virt_count = virtual_energy.shape[0]
    levels = jnp.where(
        my_index >= 0, virtual_energy[jnp.clip(my_index, 0, virt_count - 1)], jnp.float32(1.0)
    )
    occupied = occupied_energy[my_orbitals]

    outgoing = make_slabs(half_integrals, domain_map, domain_index, owner_orbitals, x)
    inner = ("zl", "yl", "c", "x")
    members = size["zl"] * size["yl"] * size["c"] * size["x"]
    per_member = owners // members
    received = lax.all_to_all(
        outgoing.reshape(members, per_member * width, rows),
        inner,
        split_axis=0,
        concat_axis=0,
        tiled=True,
    )
    scaled = partial_grams(
        received.reshape(members // size["x"], list_width, per_member, width, rows)
    )
    depth = scaled.shape[2]
    sent = scaled.astype(jnp.float16).reshape(-1, depth, width)
    arrived = lax.all_to_all(sent, ("zh", "yh"), split_axis=0, concat_axis=0, tiled=True)
    power = arrived[:, depth - 1 :, :].astype(F32) - TOP_POWER
    blocks = jnp.sum(arrived[:, : depth - 8, :].astype(F32) * jnp.exp2(power), axis=0)

    place = jnp.stack([position["yh"], x]).astype(jnp.int32)
    slices = pair_terms(blocks, levels, packed, occupied, place)
    slices = lax.all_to_all(slices, "x", split_axis=0, concat_axis=0, tiled=True)
    planes = plane_terms(slices)
    parts = lax.all_to_all(planes, "yh", split_axis=0, concat_axis=0, tiled=True)
    lines = owner_terms(parts, owners)
    all_lines = lax.all_to_all(
        lines, ("zh", "zl", "yl", "c"), split_axis=0, concat_axis=0, tiled=True
    )
    amplitude, pair_energy = join_amplitudes(parts, pair_slots, place, share)
    domain_grad = sum_grads(all_lines, line_owner, occ_local)
    return (amplitude, pair_energy, domain_grad)


def solution(mesh):
    fine = jax.sharding.Mesh(mesh.devices.reshape(4, 2, 4, 2, 2, 4), AXES)
    aux, orb = AXES[:-1], "x"
    placed = (
        P(orb, aux, None),
        P(orb, None, None),
        P(),
        P(),
        P(aux, None),
        P(aux),
        P(),
        P(),
    )
    return jax.shard_map(
        on_device,
        mesh=fine,
        in_specs=placed,
        out_specs=(P(AXES, None, None), P(AXES), P(orb, None)),
        check_vma=False,
    )
```

```python
import functools

import jax
import jax.numpy as jnp
from jax import lax
from jax.experimental import pallas as pl
from jax.experimental.pallas import tpu as pltpu
from jax.sharding import PartitionSpec as P

F32 = jnp.float32
VMEM_LIMIT = 48 * 1024 * 1024
SLAB_VMEM_LIMIT = 62 * 1024 * 1024
OWNERS_PER_STEP = 32
ORBS_PER_STEP = 16
GRAMS_PER_STEP = 2
AXES = ("zh", "zl", "yh", "yl", "c", "x")
BLOCKS = tuple((s, t) for s in range(4) for t in range(s, 4))
CROSS = tuple((s, t) for s, t in BLOCKS if s < t)
SENT = len(CROSS) + 2
TAIL = 16
TOP_POWER = 14.0


def slab_kernel(owner_list, group, integral_ref, map_ref, index_ref, out_ref, slab_ref):
    orbs = integral_ref.shape[0]
    occ_local = slab_ref.shape[0]
    per_step = out_ref.shape[0]
    step = pl.program_id(0)
    first_write = occ_local // orbs
    first_orb = group[0] * occ_local

    @pl.when(step < first_write)
    def _():
        for k in range(orbs):
            orb = step * orbs + k
            live = index_ref[pl.ds(first_orb + orb, 1), :] >= 0
            masked = map_ref[k] * live.astype(F32).astype(jnp.bfloat16)
            slab_ref[orb] = lax.dot_general(
                masked.T, integral_ref[k], (((1,), (1,)), ((), ())), preferred_element_type=F32
            ).astype(jnp.bfloat16)

    @pl.when(step >= first_write)
    def _():
        part = step - first_write
        base = jnp.right_shift(part, 1) * 16 + jnp.bitwise_and(part, 1) * 2
        for k in range(per_step):
            owner = base + (k % 4) * 32 + (k // 4 % 4) * 4 + k // 16
            out_ref[k] = slab_ref[owner_list[group[0], owner] - first_orb]


def make_slabs(half_integrals, domain_map, domain_index, owner_orbitals, orb_group):
    occ_local, rows, width = half_integrals.shape
    owners = owner_orbitals.shape[0]
    parts = occ_local // ORBS_PER_STEP
    read = lambda i, s, t: (jnp.minimum(i, parts - 1), 0, 0)
    return pl.pallas_call(
        slab_kernel,
        out_shape=jax.ShapeDtypeStruct((owners, width, rows), jnp.bfloat16),
        grid_spec=pltpu.PrefetchScalarGridSpec(
            num_scalar_prefetch=2,
            grid=(parts + owners // OWNERS_PER_STEP,),
            in_specs=[
                pl.BlockSpec((ORBS_PER_STEP, rows, width), read),
                pl.BlockSpec((ORBS_PER_STEP, width, width), read),
                pl.BlockSpec(domain_index.shape, lambda i, s, t: (0, 0)),
            ],
            out_specs=pl.BlockSpec(
                (OWNERS_PER_STEP, width, rows), lambda i, s, t: (jnp.maximum(i - parts, 0), 0, 0)
            ),
            scratch_shapes=[pltpu.VMEM((occ_local, width, rows), jnp.bfloat16)],
        ),
        compiler_params=pltpu.CompilerParams(vmem_limit_bytes=SLAB_VMEM_LIMIT),
        name="slabs",
    )(
        owner_orbitals.T,
        orb_group[None].astype(jnp.int32),
        half_integrals,
        domain_map,
        domain_index,
    )


def gram_kernel(slab_ref, out_ref):
    count, list_width, owners, width, rows = slab_ref.shape
    half = list_width * width // 2
    middle = list_width // 2
    product = functools.partial(
        lax.dot_general,
        dimension_numbers=(((1,), (1,)), ((), ())),
        preferred_element_type=F32,
    )
    pieces = out_ref.shape[1]
    depth = width // pieces
    base = SENT * depth
    line = lax.broadcasted_iota(jnp.int32, (width, width), 0)
    lane = lax.broadcasted_iota(jnp.int32, (width, width), 1)
    for j in range(owners):
        low = jnp.concatenate(
            [slab_ref[k, :middle, j].reshape(half, rows) for k in range(count)], axis=1
        )
        high = jnp.concatenate(
            [slab_ref[k, middle:, j].reshape(half, rows) for k in range(count)], axis=1
        )
        parts = (product(low, low), product(low, high), product(high, high))

        def block_at(left, right):
            row, column = left % 2 * width, right % 2 * width
            return parts[left // 2 + right // 2][row : row + width, column : column + width]

        top = jnp.zeros((8, width), F32)
        for s in range(list_width):
            top = jnp.maximum(
                top, jnp.max(jnp.abs(block_at(s, s)).reshape(width // 8, 8, width), axis=0)
            )
        top = jnp.max(jnp.max(top, axis=0, keepdims=True), axis=1, keepdims=True)
        power = jnp.clip(jnp.ceil(jnp.log2(jnp.maximum(top, 1e-35))), -100.0, 100.0)
        power = jnp.broadcast_to(power, (8, width))
        scale = jnp.exp2(TOP_POWER - power)[0:1]
        blocks = [block_at(left, right) for left, right in CROSS]
        diagonals = []
        for s in range(0, list_width, 2):
            lower = block_at(s + 1, s + 1)
            blocks.append(jnp.where(lane >= line, block_at(s, s), lower))
            diagonals.append(
                jnp.sum(jnp.where(lane == line, lower, 0.0), axis=0, keepdims=True) * scale
            )
        tail = jnp.concatenate(diagonals + [power[: 8 - len(diagonals)]], axis=0)
        for index, block in enumerate(blocks):
            block = block * scale
            for q in range(pieces):
                out_ref[j, q, index * depth : (index + 1) * depth, :] = block[
                    q * depth : (q + 1) * depth
                ]
        for q in range(pieces):
            out_ref[j, q, base : base + 8, :] = tail
            out_ref[j, q, base + 8 : base + TAIL, :] = power


def partial_grams(slabs):
    count, list_width, owners, width, rows = slabs.shape
    pieces = 4
    depth = SENT * (width // pieces) + TAIL
    return pl.pallas_call(
        gram_kernel,
        out_shape=jax.ShapeDtypeStruct((owners, pieces, depth, width), F32),
        grid=(owners // GRAMS_PER_STEP,),
        in_specs=[
            pl.BlockSpec(
                (count, list_width, GRAMS_PER_STEP, width, rows), lambda j: (0, 0, j, 0, 0)
            )
        ],
        out_specs=pl.BlockSpec((GRAMS_PER_STEP, pieces, depth, width), lambda j: (j, 0, 0, 0)),
        compiler_params=pltpu.CompilerParams(vmem_limit_bytes=VMEM_LIMIT),
        name="partial_grams",
    )(slabs)


def split(value):
    high = value.astype(jnp.bfloat16).astype(F32)
    middle = (value - high).astype(jnp.bfloat16).astype(F32)
    return [high, middle, value - high - middle]


def pair_kernel(
    packed,
    occupied,
    place,
    block_ref,
    level_ref,
    out_ref,
    ratio_ref,
    column_ref,
    place_ref,
    acc_ref,
    weight_table,
    energy_table,
):
    list_width, width = level_ref.shape
    depth = (block_ref.shape[0] - 8) // SENT
    pairs = packed.shape[0]
    piece = place[0]
    rows = pl.ds(pl.multiple_of(piece * depth, depth), depth)
    for k in range(list_width * list_width):
        weight_table[k] = 0
    for pair in range(pairs):
        weight_table[packed[pair, 0] * list_width + packed[pair, 1]] = packed[pair, 2]
    for s in range(list_width):
        column_ref[s] = jnp.broadcast_to(level_ref[s : s + 1, :], (width, width)).T
    acc_ref[...] = jnp.zeros_like(acc_ref)
    place_ref[...] = jnp.zeros_like(place_ref)
    row_squares = [jnp.zeros((depth, width), F32) for _ in range(list_width)]
    line = lax.broadcasted_iota(jnp.int32, (depth, width), 0) + piece * depth
    column = lax.broadcasted_iota(jnp.int32, (depth, width), 1)

    def block_at(index):
        return block_ref[index * depth : (index + 1) * depth, :]

    for index, (left, right) in enumerate(BLOCKS):
        if left != right:
            block = block_at(CROSS.index((left, right)))
        else:
            block = block_at(len(CROSS) + left // 2)
            if left % 2 == 0:
                block = jnp.where(column >= line, block, 0.0)
            else:
                row = SENT * depth + left // 2
                inner = jnp.where(column == line, block_ref[row : row + 1, :], 0.0)
                block = jnp.where(column < line, block, inner)
        denominator = (
            column_ref[left, rows, :]
            + level_ref[right : right + 1, :]
            - occupied[left]
            - occupied[right]
        )
        ratio = block / denominator
        ratio_ref[index] = ratio
        times = jnp.where(column == line, 1.0, 2.0) if left == right else 1.0
        energy_table[index] = jnp.sum(times * block * ratio)
        weight = weight_table[left * list_width + right]
        if left != right:
            weight = weight + weight_table[right * list_width + left]
        squares = times * (weight.astype(F32) / width) * (ratio * ratio)
        row_squares[left] = row_squares[left] + squares
        acc_ref[right : right + 1, :] += jnp.sum(squares, axis=0, keepdims=True)
    for s in range(list_width):
        place_ref[rows, :] = row_squares[s]
        acc_ref[s : s + 1, :] += jnp.sum(place_ref[...].T, axis=0, keepdims=True)

    def block_of(pair):
        low = jnp.minimum(packed[pair, 0], packed[pair, 1])
        high = jnp.maximum(packed[pair, 0], packed[pair, 1])
        return jnp.where(low == 0, 0, jnp.where(low == 1, 3, jnp.where(low == 2, 5, 6))) + high

    lane = lax.broadcasted_iota(jnp.int32, (1, width), 1)
    energies = jnp.zeros((1, width), F32)
    for pair in range(pairs):
        energy = -packed[pair, 2].astype(F32) * energy_table[block_of(pair)] / (width * width)
        energies = jnp.where(lane == pair, energy, energies)
    share = pairs // list_width
    for quarter in range(list_width):
        lines = split(acc_ref[quarter : quarter + 1, :]) + split(energies)
        lines.append(jnp.zeros((TAIL - len(lines), width), F32))
        tail = jnp.concatenate(lines, axis=0).astype(jnp.bfloat16)
        out_ref[quarter, share * depth :, :] = tail
    for pair in range(pairs):
        quarter, k = pair // share, pair % share
        live = (packed[pair, 2] > 0).astype(F32)
        value = (-ratio_ref[block_of(pair)] * live).astype(jnp.bfloat16)
        out_ref[quarter, k * depth : (k + 1) * depth, :] = value


def pair_terms(blocks, levels, packed, occupied, place):
    height, width = blocks.shape
    depth = (height - 8) // SENT
    list_width = levels.shape[0]
    whole = pl.BlockSpec(memory_space=pltpu.VMEM)
    scalar = pl.BlockSpec(memory_space=pltpu.SMEM)
    rows = packed.shape[0] // list_width * depth + TAIL
    return pl.pallas_call(
        pair_kernel,
        out_shape=jax.ShapeDtypeStruct((list_width, rows, width), jnp.bfloat16),
        in_specs=[scalar, scalar, scalar, whole, whole],
        out_specs=whole,
        scratch_shapes=[
            pltpu.VMEM((len(BLOCKS), depth, width), F32),
            pltpu.VMEM((list_width, width, width), F32),
            pltpu.VMEM((width, width), F32),
            pltpu.VMEM((list_width, width), F32),
            pltpu.SMEM((list_width * list_width,), jnp.int32),
            pltpu.SMEM((len(BLOCKS),), F32),
        ],
        compiler_params=pltpu.CompilerParams(vmem_limit_bytes=VMEM_LIMIT),
        name="pair_terms",
    )(packed, occupied, place, blocks, levels)


def plane_kernel(parts_ref, out_ref):
    owners, height, width = parts_ref.shape
    body = height - TAIL
    tails = [parts_ref[s, body:, :].astype(F32) for s in range(owners)]
    vectors = [tails[s][k : k + 1] for k in range(3) for s in range(owners)]
    for s in range(owners):
        lines = vectors + [tails[s][3:6], jnp.zeros((TAIL - 3 * owners - 3, width), F32)]
        tail = jnp.concatenate(lines, axis=0).astype(jnp.bfloat16)
        out_ref[s, :body, :] = parts_ref[s, :body, :]
        out_ref[s, body:, :] = tail


def plane_terms(parts):
    whole = pl.BlockSpec(memory_space=pltpu.VMEM)
    return pl.pallas_call(
        plane_kernel,
        out_shape=jax.ShapeDtypeStruct(parts.shape, parts.dtype),
        in_specs=[whole],
        out_specs=whole,
        compiler_params=pltpu.CompilerParams(vmem_limit_bytes=VMEM_LIMIT),
        name="plane_terms",
    )(parts)


def owner_kernel(parts_ref, terms_ref):
    pieces, height, width = parts_ref.shape
    total = None
    for q in range(pieces):
        tail = parts_ref[q, height - TAIL :, :].astype(F32)
        vectors = tail[0:4] + (tail[4:8] + tail[8:12])
        total = vectors if total is None else total + vectors
    tile = jnp.concatenate([total, total], axis=0)
    for k in range(terms_ref.shape[0] // 8):
        terms_ref[8 * k : 8 * k + 8, :] = tile


def owner_terms(parts, lines):
    whole = pl.BlockSpec(memory_space=pltpu.VMEM)
    return pl.pallas_call(
        owner_kernel,
        out_shape=jax.ShapeDtypeStruct((lines, parts.shape[2]), F32),
        in_specs=[whole],
        out_specs=whole,
        compiler_params=pltpu.CompilerParams(vmem_limit_bytes=VMEM_LIMIT),
        name="owner_terms",
    )(parts)


def join_kernel(slots, place, parts_ref, out_ref, energy_ref):
    share, width, _ = out_ref.shape
    sources, height, _ = parts_ref.shape
    depth = (height - TAIL) // share
    line = lax.broadcasted_iota(jnp.int32, (width, width), 0)
    column = lax.broadcasted_iota(jnp.int32, (width, width), 1)
    energies = jnp.zeros((1, width), F32)
    for q in range(sources):
        tail = parts_ref[q, height - TAIL :, :].astype(F32)
        energies = energies + (tail[12:13] + (tail[13:14] + tail[14:15]))
    for k in range(share):
        block = jnp.concatenate(
            [
                parts_ref[q, k * depth : (k + 1) * depth, :].astype(F32)
                for q in range(sources)
            ],
            axis=0,
        )
        pair = place[1] * share + k
        swapped = slots[0, pair] > slots[1, pair]
        same = slots[0, pair] == slots[1, pair]
        other = block.T
        both = jnp.where(line == column, block, block + other)
        value = jnp.where(same, both, jnp.where(swapped, other, block))
        out_ref[k] = value.astype(jnp.bfloat16)
        energy_ref[k] = jnp.sum(jnp.where(column[0:1] == pair, energies, 0.0))


def join_amplitudes(parts, pair_slots, place, share):
    whole = pl.BlockSpec(memory_space=pltpu.VMEM)
    scalar = pl.BlockSpec(memory_space=pltpu.SMEM)
    width = parts.shape[2]
    return pl.pallas_call(
        join_kernel,
        out_shape=(
            jax.ShapeDtypeStruct((share, width, width), jnp.bfloat16),
            jax.ShapeDtypeStruct((share,), F32),
        ),
        in_specs=[scalar, scalar, whole],
        out_specs=(whole, scalar),
        compiler_params=pltpu.CompilerParams(vmem_limit_bytes=VMEM_LIMIT),
        name="join_amplitudes",
    )(pair_slots, place, parts)


def grad_kernel(owner_ref, terms_ref, out_ref):
    occ_local = out_ref.shape[0]
    lines = owner_ref.shape[1]
    chosen = (
        lax.broadcasted_iota(jnp.int32, (occ_local, lines), 0) == owner_ref[...]
    ).astype(F32)
    out_ref[...] = jnp.dot(
        chosen, terms_ref[...], preferred_element_type=F32, precision=lax.Precision.HIGHEST
    )


def sum_grads(terms, line_owner, occ_local):
    whole = pl.BlockSpec(memory_space=pltpu.VMEM)
    return pl.pallas_call(
        grad_kernel,
        out_shape=jax.ShapeDtypeStruct((occ_local, terms.shape[1]), F32),
        in_specs=[whole, whole],
        out_specs=whole,
        compiler_params=pltpu.CompilerParams(vmem_limit_bytes=VMEM_LIMIT),
        name="sum_grads",
    )(line_owner, terms)


def on_device(
    half_integrals,
    domain_map,
    domain_index,
    owner_orbitals,
    pair_slots,
    pair_weight,
    virtual_energy,
    occupied_energy,
):
    position = {name: lax.axis_index(name) for name in AXES}
    size = {name: lax.axis_size(name) for name in AXES}
    x = position["x"]

    def aux_rank(yh):
        rank = 0
        for name in AXES[:-1]:
            rank = rank * size[name] + (yh if name == "yh" else position[name])
        return rank

    occ_local, rows, width = half_integrals.shape
    owners, list_width = owner_orbitals.shape
    share = pair_slots.shape[0] // size["x"]
    cross = [(q * 4 + s, s * 4 + q) for q in range(4) for s in range(4)]

    packed = lax.ppermute(
        jnp.concatenate([pair_slots, pair_weight[:, None]], axis=1), ("yh", "x"), cross
    )
    own = lax.dynamic_slice_in_dim(owner_orbitals, x, 1, 1)[:, 0] - x * occ_local
    grid = own.reshape([size[name] for name in AXES[:-1]])
    line_owner = grid.transpose(0, 1, 3, 4, 2).reshape(1, -1)

    my_orbitals = lax.dynamic_slice_in_dim(owner_orbitals, aux_rank(x), 1, 0)[0]
    my_index = domain_index[my_orbitals]
    virt_count = virtual_energy.shape[0]
    levels = jnp.where(
        my_index >= 0, virtual_energy[jnp.clip(my_index, 0, virt_count - 1)], jnp.float32(1.0)
    )
    occupied = occupied_energy[my_orbitals]
    levels, line_owner = lax.optimization_barrier((levels, line_owner))

    outgoing = make_slabs(half_integrals, domain_map, domain_index, owner_orbitals, x)
    inner = ("zl", "yl", "c", "x")
    members = size["zl"] * size["yl"] * size["c"] * size["x"]
    per_member = owners // members
    received = lax.all_to_all(
        outgoing.reshape(members, per_member * width, rows),
        inner,
        split_axis=0,
        concat_axis=0,
        tiled=True,
    )
    scaled = partial_grams(
        received.reshape(members // size["x"], list_width, per_member, width, rows)
    )
    depth = scaled.shape[2]
    sent = scaled.astype(jnp.float16).reshape(-1, depth, width)
    arrived = lax.all_to_all(sent, ("zh", "yh"), split_axis=0, concat_axis=0, tiled=True)
    power = arrived[:, depth - 1 :, :].astype(F32) - TOP_POWER
    blocks = jnp.sum(arrived[:, : depth - 8, :].astype(F32) * jnp.exp2(power), axis=0)

    place = jnp.stack([position["yh"], x]).astype(jnp.int32)
    slices = pair_terms(blocks, levels, packed, occupied, place)
    slices = lax.all_to_all(slices, "x", split_axis=0, concat_axis=0, tiled=True)
    planes = plane_terms(slices)
    parts = lax.all_to_all(planes, "yh", split_axis=0, concat_axis=0, tiled=True)
    lines = owner_terms(parts, owners)
    amplitude, pair_energy = join_amplitudes(parts, pair_slots.T, place, share)
    lines, amplitude = lax.optimization_barrier((lines, amplitude))
    all_lines = lax.all_to_all(
        lines, ("zh", "zl", "yl", "c"), split_axis=0, concat_axis=0, tiled=True
    )
    domain_grad = sum_grads(all_lines, line_owner, occ_local)
    return (amplitude, pair_energy, domain_grad)


def solution(mesh):
    fine = jax.sharding.Mesh(mesh.devices.reshape(4, 2, 4, 2, 2, 4), AXES)
    aux, orb = AXES[:-1], "x"
    placed = (
        P(orb, aux, None),
        P(orb, None, None),
        P(),
        P(),
        P(aux, None),
        P(aux),
        P(),
        P(),
    )
    return jax.shard_map(
        on_device,
        mesh=fine,
        in_specs=placed,
        out_specs=(P(AXES, None, None), P(AXES), P(orb, None)),
        check_vma=False,
    )
```

```python
import functools

import jax
import jax.numpy as jnp
from jax import lax
from jax.experimental import pallas as pl
from jax.experimental.pallas import tpu as pltpu
from jax.sharding import PartitionSpec as P

F32 = jnp.float32
VMEM_LIMIT = 48 * 1024 * 1024
SLAB_VMEM_LIMIT = 62 * 1024 * 1024
OWNERS_PER_STEP = 32
ORBS_PER_STEP = 16
GRAMS_PER_STEP = 2
AXES = ("zh", "zl", "yh", "yl", "c", "x")
BLOCKS = tuple((s, t) for s in range(4) for t in range(s, 4))
CROSS = tuple((s, t) for s, t in BLOCKS if s < t)
SENT = len(CROSS) + 2
TAIL = 16
TOP_POWER = 14.0


def slab_kernel(owner_list, group, integral_ref, map_ref, index_ref, out_ref, slab_ref):
    orbs = integral_ref.shape[0]
    occ_local = slab_ref.shape[0]
    per_step = out_ref.shape[0]
    step = pl.program_id(0)
    first_write = occ_local // orbs
    first_orb = group[0] * occ_local

    @pl.when(step < first_write)
    def _():
        for k in range(orbs):
            orb = step * orbs + k
            live = index_ref[pl.ds(first_orb + orb, 1), :] >= 0
            masked = map_ref[k] * live.astype(F32).astype(jnp.bfloat16)
            slab_ref[orb] = lax.dot_general(
                masked.T, integral_ref[k], (((1,), (1,)), ((), ())), preferred_element_type=F32
            ).astype(jnp.bfloat16)

    @pl.when(step >= first_write)
    def _():
        part = step - first_write
        base = jnp.right_shift(part, 1) * 16 + jnp.bitwise_and(part, 1) * 2
        for k in range(per_step):
            owner = base + (k % 4) * 32 + (k // 4 % 4) * 4 + k // 16
            out_ref[k] = slab_ref[owner_list[group[0], owner] - first_orb]


def make_slabs(half_integrals, domain_map, domain_index, owner_orbitals, orb_group):
    occ_local, rows, width = half_integrals.shape
    owners = owner_orbitals.shape[0]
    parts = occ_local // ORBS_PER_STEP
    read = lambda i, s, t: (jnp.minimum(i, parts - 1), 0, 0)
    return pl.pallas_call(
        slab_kernel,
        out_shape=jax.ShapeDtypeStruct((owners, width, rows), jnp.bfloat16),
        grid_spec=pltpu.PrefetchScalarGridSpec(
            num_scalar_prefetch=2,
            grid=(parts + owners // OWNERS_PER_STEP,),
            in_specs=[
                pl.BlockSpec((ORBS_PER_STEP, rows, width), read),
                pl.BlockSpec((ORBS_PER_STEP, width, width), read),
                pl.BlockSpec(domain_index.shape, lambda i, s, t: (0, 0)),
            ],
            out_specs=pl.BlockSpec(
                (OWNERS_PER_STEP, width, rows), lambda i, s, t: (jnp.maximum(i - parts, 0), 0, 0)
            ),
            scratch_shapes=[pltpu.VMEM((occ_local, width, rows), jnp.bfloat16)],
        ),
        compiler_params=pltpu.CompilerParams(vmem_limit_bytes=SLAB_VMEM_LIMIT),
        name="slabs",
    )(
        owner_orbitals.T,
        orb_group[None].astype(jnp.int32),
        half_integrals,
        domain_map,
        domain_index,
    )


def gram_kernel(slab_ref, out_ref):
    count, list_width, owners, width, rows = slab_ref.shape
    half = list_width * width // 2
    middle = list_width // 2
    product = functools.partial(
        lax.dot_general,
        dimension_numbers=(((1,), (1,)), ((), ())),
        preferred_element_type=F32,
    )
    pieces = out_ref.shape[1]
    depth = width // pieces
    base = SENT * depth
    line = lax.broadcasted_iota(jnp.int32, (width, width), 0)
    lane = lax.broadcasted_iota(jnp.int32, (width, width), 1)
    for j in range(owners):
        low = jnp.concatenate(
            [slab_ref[k, :middle, j].reshape(half, rows) for k in range(count)], axis=1
        )
        high = jnp.concatenate(
            [slab_ref[k, middle:, j].reshape(half, rows) for k in range(count)], axis=1
        )
        parts = (product(low, low), product(low, high), product(high, high))

        def block_at(left, right):
            row, column = left % 2 * width, right % 2 * width
            return parts[left // 2 + right // 2][row : row + width, column : column + width]

        top = jnp.zeros((8, width), F32)
        for s in range(list_width):
            top = jnp.maximum(
                top, jnp.max(jnp.abs(block_at(s, s)).reshape(width // 8, 8, width), axis=0)
            )
        top = jnp.max(jnp.max(top, axis=0, keepdims=True), axis=1, keepdims=True)
        power = jnp.clip(jnp.ceil(jnp.log2(jnp.maximum(top, 1e-35))), -100.0, 100.0)
        power = jnp.broadcast_to(power, (8, width))
        scale = jnp.exp2(TOP_POWER - power)[0:1]
        blocks = [block_at(left, right) for left, right in CROSS]
        diagonals = []
        for s in range(0, list_width, 2):
            lower = block_at(s + 1, s + 1)
            blocks.append(jnp.where(lane >= line, block_at(s, s), lower))
            diagonals.append(
                jnp.sum(jnp.where(lane == line, lower, 0.0), axis=0, keepdims=True) * scale
            )
        tail = jnp.concatenate(diagonals + [power[: 8 - len(diagonals)]], axis=0)
        for index, block in enumerate(blocks):
            block = block * scale
            for q in range(pieces):
                out_ref[j, q, index * depth : (index + 1) * depth, :] = block[
                    q * depth : (q + 1) * depth
                ]
        for q in range(pieces):
            out_ref[j, q, base : base + 8, :] = tail
            out_ref[j, q, base + 8 : base + TAIL, :] = power


def partial_grams(slabs):
    count, list_width, owners, width, rows = slabs.shape
    pieces = 4
    depth = SENT * (width // pieces) + TAIL
    return pl.pallas_call(
        gram_kernel,
        out_shape=jax.ShapeDtypeStruct((owners, pieces, depth, width), F32),
        grid=(owners // GRAMS_PER_STEP,),
        in_specs=[
            pl.BlockSpec(
                (count, list_width, GRAMS_PER_STEP, width, rows), lambda j: (0, 0, j, 0, 0)
            )
        ],
        out_specs=pl.BlockSpec((GRAMS_PER_STEP, pieces, depth, width), lambda j: (j, 0, 0, 0)),
        compiler_params=pltpu.CompilerParams(vmem_limit_bytes=VMEM_LIMIT),
        name="partial_grams",
    )(slabs)


def split(value):
    high = value.astype(jnp.bfloat16).astype(F32)
    middle = (value - high).astype(jnp.bfloat16).astype(F32)
    return [high, middle, value - high - middle]


def pair_kernel(
    packed,
    occupied,
    place,
    block_ref,
    level_ref,
    out_ref,
    ratio_ref,
    column_ref,
    place_ref,
    acc_ref,
    weight_table,
    energy_table,
):
    list_width, width = level_ref.shape
    depth = (block_ref.shape[0] - 8) // SENT
    pairs = packed.shape[0]
    piece = place[0]
    rows = pl.ds(pl.multiple_of(piece * depth, depth), depth)
    for k in range(list_width * list_width):
        weight_table[k] = 0
    for pair in range(pairs):
        weight_table[packed[pair, 0] * list_width + packed[pair, 1]] = packed[pair, 2]
    for s in range(list_width):
        column_ref[s] = jnp.broadcast_to(level_ref[s : s + 1, :], (width, width)).T
    acc_ref[...] = jnp.zeros_like(acc_ref)
    place_ref[...] = jnp.zeros_like(place_ref)
    row_squares = [jnp.zeros((depth, width), F32) for _ in range(list_width)]
    line = lax.broadcasted_iota(jnp.int32, (depth, width), 0) + piece * depth
    column = lax.broadcasted_iota(jnp.int32, (depth, width), 1)

    def block_at(index):
        return block_ref[index * depth : (index + 1) * depth, :]

    for index, (left, right) in enumerate(BLOCKS):
        if left != right:
            block = block_at(CROSS.index((left, right)))
        else:
            block = block_at(len(CROSS) + left // 2)
            if left % 2 == 0:
                block = jnp.where(column >= line, block, 0.0)
            else:
                row = SENT * depth + left // 2
                inner = jnp.where(column == line, block_ref[row : row + 1, :], 0.0)
                block = jnp.where(column < line, block, inner)
        denominator = (
            column_ref[left, rows, :]
            + level_ref[right : right + 1, :]
            - occupied[left]
            - occupied[right]
        )
        ratio = block / denominator
        ratio_ref[index] = ratio
        times = jnp.where(column == line, 1.0, 2.0) if left == right else 1.0
        energy_table[index] = jnp.sum(times * block * ratio)
        weight = weight_table[left * list_width + right]
        if left != right:
            weight = weight + weight_table[right * list_width + left]
        squares = times * (weight.astype(F32) / width) * (ratio * ratio)
        row_squares[left] = row_squares[left] + squares
        acc_ref[right : right + 1, :] += jnp.sum(squares, axis=0, keepdims=True)
    for s in range(list_width):
        place_ref[rows, :] = row_squares[s]
        acc_ref[s : s + 1, :] += jnp.sum(place_ref[...].T, axis=0, keepdims=True)

    def block_of(pair):
        low = jnp.minimum(packed[pair, 0], packed[pair, 1])
        high = jnp.maximum(packed[pair, 0], packed[pair, 1])
        return jnp.where(low == 0, 0, jnp.where(low == 1, 3, jnp.where(low == 2, 5, 6))) + high

    lane = lax.broadcasted_iota(jnp.int32, (1, width), 1)
    energies = jnp.zeros((1, width), F32)
    for pair in range(pairs):
        energy = -packed[pair, 2].astype(F32) * energy_table[block_of(pair)] / (width * width)
        energies = jnp.where(lane == pair, energy, energies)
    share = pairs // list_width
    for quarter in range(list_width):
        lines = split(acc_ref[quarter : quarter + 1, :]) + split(energies)
        lines.append(jnp.zeros((TAIL - len(lines), width), F32))
        tail = jnp.concatenate(lines, axis=0).astype(jnp.bfloat16)
        out_ref[quarter, share * depth :, :] = tail
    for pair in range(pairs):
        quarter, k = pair // share, pair % share
        live = (packed[pair, 2] > 0).astype(F32)
        value = (-ratio_ref[block_of(pair)] * live).astype(jnp.bfloat16)
        out_ref[quarter, k * depth : (k + 1) * depth, :] = value


def pair_terms(blocks, levels, packed, occupied, place):
    height, width = blocks.shape
    depth = (height - 8) // SENT
    list_width = levels.shape[0]
    whole = pl.BlockSpec(memory_space=pltpu.VMEM)
    scalar = pl.BlockSpec(memory_space=pltpu.SMEM)
    rows = packed.shape[0] // list_width * depth + TAIL
    return pl.pallas_call(
        pair_kernel,
        out_shape=jax.ShapeDtypeStruct((list_width, rows, width), jnp.bfloat16),
        in_specs=[scalar, scalar, scalar, whole, whole],
        out_specs=whole,
        scratch_shapes=[
            pltpu.VMEM((len(BLOCKS), depth, width), F32),
            pltpu.VMEM((list_width, width, width), F32),
            pltpu.VMEM((width, width), F32),
            pltpu.VMEM((list_width, width), F32),
            pltpu.SMEM((list_width * list_width,), jnp.int32),
            pltpu.SMEM((len(BLOCKS),), F32),
        ],
        compiler_params=pltpu.CompilerParams(vmem_limit_bytes=VMEM_LIMIT),
        name="pair_terms",
    )(packed, occupied, place, blocks, levels)


def plane_kernel(parts_ref, out_ref):
    owners, height, width = parts_ref.shape
    body = height - TAIL
    tails = [parts_ref[s, body:, :].astype(F32) for s in range(owners)]
    vectors = [tails[s][k : k + 1] for k in range(3) for s in range(owners)]
    for s in range(owners):
        lines = vectors + [tails[s][3:6], jnp.zeros((TAIL - 3 * owners - 3, width), F32)]
        tail = jnp.concatenate(lines, axis=0).astype(jnp.bfloat16)
        out_ref[s, :body, :] = parts_ref[s, :body, :]
        out_ref[s, body:, :] = tail


def plane_terms(parts):
    whole = pl.BlockSpec(memory_space=pltpu.VMEM)
    return pl.pallas_call(
        plane_kernel,
        out_shape=jax.ShapeDtypeStruct(parts.shape, parts.dtype),
        in_specs=[whole],
        out_specs=whole,
        compiler_params=pltpu.CompilerParams(vmem_limit_bytes=VMEM_LIMIT),
        name="plane_terms",
    )(parts)


def owner_kernel(parts_ref, terms_ref):
    pieces, height, width = parts_ref.shape
    total = None
    for q in range(pieces):
        tail = parts_ref[q, height - TAIL :, :].astype(F32)
        vectors = tail[0:4] + (tail[4:8] + tail[8:12])
        total = vectors if total is None else total + vectors
    tile = jnp.concatenate([total, total], axis=0)
    for k in range(terms_ref.shape[0] // 8):
        terms_ref[8 * k : 8 * k + 8, :] = tile


def owner_terms(parts, lines):
    whole = pl.BlockSpec(memory_space=pltpu.VMEM)
    return pl.pallas_call(
        owner_kernel,
        out_shape=jax.ShapeDtypeStruct((lines, parts.shape[2]), F32),
        in_specs=[whole],
        out_specs=whole,
        compiler_params=pltpu.CompilerParams(vmem_limit_bytes=VMEM_LIMIT),
        name="owner_terms",
    )(parts)


def join_kernel(slots, place, parts_ref, out_ref, energy_ref):
    share, width, _ = out_ref.shape
    sources, height, _ = parts_ref.shape
    depth = (height - TAIL) // share
    line = lax.broadcasted_iota(jnp.int32, (width, width), 0)
    column = lax.broadcasted_iota(jnp.int32, (width, width), 1)
    energies = jnp.zeros((1, width), F32)
    for q in range(sources):
        tail = parts_ref[q, height - TAIL :, :].astype(F32)
        energies = energies + (tail[12:13] + (tail[13:14] + tail[14:15]))
    for k in range(share):
        block = jnp.concatenate(
            [
                parts_ref[q, k * depth : (k + 1) * depth, :].astype(F32)
                for q in range(sources)
            ],
            axis=0,
        )
        pair = place[1] * share + k
        swapped = slots[0, pair] > slots[1, pair]
        same = slots[0, pair] == slots[1, pair]
        other = block.T
        both = jnp.where(line == column, block, block + other)
        value = jnp.where(same, both, jnp.where(swapped, other, block))
        out_ref[k] = value.astype(jnp.bfloat16)
        energy_ref[k] = jnp.sum(jnp.where(column[0:1] == pair, energies, 0.0))


def join_amplitudes(parts, pair_slots, place, share):
    whole = pl.BlockSpec(memory_space=pltpu.VMEM)
    scalar = pl.BlockSpec(memory_space=pltpu.SMEM)
    width = parts.shape[2]
    return pl.pallas_call(
        join_kernel,
        out_shape=(
            jax.ShapeDtypeStruct((share, width, width), jnp.bfloat16),
            jax.ShapeDtypeStruct((share,), F32),
        ),
        in_specs=[scalar, scalar, whole],
        out_specs=(whole, scalar),
        compiler_params=pltpu.CompilerParams(vmem_limit_bytes=VMEM_LIMIT),
        name="join_amplitudes",
    )(pair_slots, place, parts)


def grad_kernel(owner_ref, terms_ref, out_ref):
    occ_local = out_ref.shape[0]
    lines = owner_ref.shape[1]
    chosen = (
        lax.broadcasted_iota(jnp.int32, (occ_local, lines), 0) == owner_ref[...]
    ).astype(F32)
    out_ref[...] = jnp.dot(
        chosen, terms_ref[...], preferred_element_type=F32, precision=lax.Precision.HIGHEST
    )


def sum_grads(terms, line_owner, occ_local):
    whole = pl.BlockSpec(memory_space=pltpu.VMEM)
    return pl.pallas_call(
        grad_kernel,
        out_shape=jax.ShapeDtypeStruct((occ_local, terms.shape[1]), F32),
        in_specs=[whole, whole],
        out_specs=whole,
        compiler_params=pltpu.CompilerParams(vmem_limit_bytes=VMEM_LIMIT),
        name="sum_grads",
    )(line_owner, terms)


def on_device(
    half_integrals,
    domain_map,
    domain_index,
    owner_orbitals,
    pair_slots,
    pair_weight,
    virtual_energy,
    occupied_energy,
):
    position = {name: lax.axis_index(name) for name in AXES}
    size = {name: lax.axis_size(name) for name in AXES}
    x = position["x"]

    def aux_rank(yh):
        rank = 0
        for name in AXES[:-1]:
            rank = rank * size[name] + (yh if name == "yh" else position[name])
        return rank

    occ_local, rows, width = half_integrals.shape
    owners, list_width = owner_orbitals.shape
    share = pair_slots.shape[0] // size["x"]
    cross = [(q * 4 + s, s * 4 + q) for q in range(4) for s in range(4)]

    packed = lax.ppermute(
        jnp.concatenate([pair_slots, pair_weight[:, None]], axis=1), ("yh", "x"), cross
    )
    own = lax.dynamic_slice_in_dim(owner_orbitals, x, 1, 1)[:, 0] - x * occ_local
    grid = own.reshape([size[name] for name in AXES[:-1]])
    line_owner = grid.transpose(0, 1, 3, 4, 2).reshape(1, -1)

    my_orbitals = lax.dynamic_slice_in_dim(owner_orbitals, aux_rank(x), 1, 0)[0]
    my_index = domain_index[my_orbitals]
    virt_count = virtual_energy.shape[0]
    levels = jnp.where(
        my_index >= 0, virtual_energy[jnp.clip(my_index, 0, virt_count - 1)], jnp.float32(1.0)
    )
    occupied = occupied_energy[my_orbitals]
    levels, line_owner = lax.optimization_barrier((levels, line_owner))

    outgoing = make_slabs(half_integrals, domain_map, domain_index, owner_orbitals, x)
    inner = ("zl", "yl", "c", "x")
    members = size["zl"] * size["yl"] * size["c"] * size["x"]
    per_member = owners // members
    received = lax.all_to_all(
        outgoing.reshape(members, per_member * width, rows),
        inner,
        split_axis=0,
        concat_axis=0,
        tiled=True,
    )
    scaled = partial_grams(
        received.reshape(members // size["x"], list_width, per_member, width, rows)
    )
    depth = scaled.shape[2]
    sent = scaled.astype(jnp.float16).reshape(-1, depth, width)
    arrived = lax.all_to_all(sent, ("zh", "yh"), split_axis=0, concat_axis=0, tiled=True)
    power = arrived[:, depth - 1 :, :].astype(F32) - TOP_POWER
    blocks = jnp.sum(arrived[:, : depth - 8, :].astype(F32) * jnp.exp2(power), axis=0)

    place = jnp.stack([position["yh"], x]).astype(jnp.int32)
    slices = pair_terms(blocks, levels, packed, occupied, place)
    slices = lax.all_to_all(slices, "x", split_axis=0, concat_axis=0, tiled=True)
    planes = plane_terms(slices)
    parts = lax.all_to_all(planes, "yh", split_axis=0, concat_axis=0, tiled=True)
    lines = owner_terms(parts, owners)
    amplitude, pair_energy = join_amplitudes(parts, pair_slots.T, place, share)
    all_lines = lax.all_to_all(
        lines, ("zh", "zl", "yl", "c"), split_axis=0, concat_axis=0, tiled=True
    )
    domain_grad = sum_grads(all_lines, line_owner, occ_local)
    return (amplitude, pair_energy, domain_grad)


def solution(mesh):
    fine = jax.sharding.Mesh(mesh.devices.reshape(4, 2, 4, 2, 2, 4), AXES)
    aux, orb = AXES[:-1], "x"
    placed = (
        P(orb, aux, None),
        P(orb, None, None),
        P(),
        P(),
        P(aux, None),
        P(aux),
        P(),
        P(),
    )
    return jax.shard_map(
        on_device,
        mesh=fine,
        in_specs=placed,
        out_specs=(P(AXES, None, None), P(AXES), P(orb, None)),
        check_vma=False,
    )
```
